256 devices in a mesh: rows: 32 (over y, x, core), cols: 8 (over z).
Axes of the slice: x: 4, y: 4, z: 8, core: 2. Of those that a mesh axis runs over, the one named last changes fastest.
Arguments:
- panel: float32 [262144, 128], P(('rows', 'cols')), may hold values from -0.095703125 to 0.095703125, as said below
- trailing: float32 [262144, 1024], P('rows', 'cols'), may hold values from -32 to 32
Outputs:
- factor_r: float32 [128, 128], replicated
- coupling: float32 [128, 1024], P(None, 'cols')
- updated: float32 [262144, 1024], P('rows', 'cols')
The draws below stay inside these ranges and needn't reach their ends.
Inputs may be any that keep to these rules, and one draw needn't show every extreme that they name: `panel`: full column rank.
All inputs are finite; a program needn't handle non-finite values.
Results may differ from the reference program's by a relative error of at most 0.0003.
Values sent between devices are 32-bit elements; how exact they have to be, the bound alone decides.
A program may use at most 64 MiB of HBM per device.

```python
import jax
import jax.numpy as jnp
from jax import lax

PANEL = 128
TRAIL = 1024
ROWS = 262144


def shaped_noise(key, shape):
    key_normal = jax.random.fold_in(key, 0)
    gaussian = jnp.clip(jax.random.normal(key_normal, shape, jnp.float32), -6.0, 6.0)
    return gaussian


def panel_values(key):
    key_noise, key_common, key_mix, key_scale = jax.random.split(key, 4)
    common = jnp.clip(jax.random.normal(key_common, (ROWS, 1), jnp.float32), -6.0, 6.0)
    mixing = jax.random.uniform(key_mix, (1, PANEL), jnp.float32, -0.5, 0.5)
    column_scale = jnp.exp(jax.random.uniform(key_scale, (1, PANEL), jnp.float32, jnp.log(0.3), jnp.log(3.0)))
    position = jnp.arange(ROWS, dtype=jnp.float32) / ROWS
    row_scale = jnp.sqrt(0.5 + 2.5 * (0.5 + (position - 0.5)))
    noise_base = shaped_noise(key_noise, (ROWS, PANEL))
    return row_scale[:, None] * column_scale * (noise_base + mixing * common)


def draw_panel(key, part):
    values = panel_values(key)
    return (values / jnp.sqrt(jnp.float32(ROWS))).astype(jnp.float32)


def draw_trailing(key, part):
    values = panel_values(key)
    key = jax.random.fold_in(key, 23)
    key_source, key_coeff, key_sign, key_noise = jax.random.split(key, 4)
    sources = jax.random.randint(key_source, (3, TRAIL), 0, PANEL)
    coeffs = jax.random.uniform(key_coeff, (3, TRAIL), jnp.float32, 0.5, 1.5)
    sign_flip = 2.0 * jax.random.randint(key_sign, (3, TRAIL), 0, 2).astype(jnp.float32) - 1.0
    coeffs = coeffs * sign_flip
    signal = jnp.zeros((ROWS, TRAIL), jnp.float32)
    for source_idx in range(3):
        signal = signal + jnp.take(values, sources[source_idx], axis=1) * coeffs[source_idx][None, :]
    noise_part = 0.5 * shaped_noise(key_noise, (ROWS, TRAIL))
    return jnp.clip(signal + noise_part, -32.0, 32.0).astype(jnp.float32)


def setup_inputs(seed: int = 0) -> dict:
    key_list = jax.random.split(jax.random.key(seed), 3)
    panel = draw_panel(jax.random.fold_in(key_list[2], 71), 0)
    trailing = draw_trailing(jax.random.fold_in(key_list[2], 71), 0)
    return dict(panel=panel, trailing=trailing)


def reference(panel, trailing):
    gram_whole = jnp.einsum('ri,rj->ij', panel, panel, precision=lax.Precision.HIGHEST)
    factor_r = jnp.linalg.cholesky(gram_whole).T
    basis_t = jax.scipy.linalg.solve_triangular(factor_r, panel.T, trans=1, lower=False)
    coupling = jnp.dot(basis_t.astype(jnp.float32), trailing.astype(jnp.float32), precision=lax.Precision.HIGHEST, preferred_element_type=jnp.float32)
    projected = jnp.einsum('kr,kj->rj', basis_t, coupling, precision=lax.Precision.HIGHEST)
    updated = trailing - projected
    return (factor_r, coupling, updated)
```

```python
import functools

import jax
import jax.numpy as jnp
from jax import lax
from jax.experimental import pallas as pl
from jax.experimental.pallas import tpu as pltpu
from jax.sharding import PartitionSpec as P

MESH = pl.DeviceIdType.MESH
HIGHEST = lax.Precision.HIGHEST
WIDTH = 128
BLOCK = 8
VMEM_LIMIT = 60 * 1024 * 1024


def split_terms(value):
    high = value.astype(jnp.bfloat16)
    low = (value - high.astype(jnp.float32)).astype(jnp.bfloat16)
    return jnp.concatenate([high, low], axis=1)


def contract_rows(left, right, precision=None):
    return lax.dot_general(
        left,
        right,
        (((0,), (0,)), ((), ())),
        precision=precision,
        preferred_element_type=jnp.float32,
    )


def eliminate(work, first, last):
    lane = lax.broadcasted_iota(jnp.int32, (BLOCK, WIDTH), 1)
    sub = lax.broadcasted_iota(jnp.int32, (BLOCK, WIDTH), 0)

    def one_block(index, carry):
        start = pl.multiple_of(index * BLOCK, BLOCK)
        rows = work[pl.ds(start, BLOCK), :]
        gram_part = rows[:, :WIDTH]
        columns = []
        for a in range(BLOCK):
            picked = jnp.where(lane == start + a, gram_part, 0.0)
            column = jnp.sum(picked, axis=1, keepdims=True)
            columns.append(jnp.broadcast_to(column, (BLOCK, WIDTH)))
        scale = jnp.zeros((BLOCK, WIDTH), jnp.float32)
        for a in range(BLOCK):
            inverse = 1.0 / jnp.broadcast_to(columns[a][a : a + 1, :], (BLOCK, WIDTH))
            scale = jnp.where(sub == a, inverse, scale)
            factor = jnp.where(sub > a, columns[a] * inverse, 0.0)
            for d in range(a + 1, BLOCK):
                pivot_row = jnp.broadcast_to(columns[d][a : a + 1, :], (BLOCK, WIDTH))
                columns[d] = columns[d] - factor * pivot_row
            pivot_row = jnp.broadcast_to(rows[a : a + 1, :], (BLOCK, 2 * WIDTH))
            rows = rows - jnp.concatenate([factor, factor], axis=1) * pivot_row
        work[pl.ds(start, BLOCK), :] = rows
        lower = jnp.where(lane >= start + BLOCK, rows[:, :WIDTH] * scale, 0.0)
        work[...] = work[...] - contract_rows(lower, rows, HIGHEST)
        return carry

    lax.fori_loop(first, last, one_block, 0)


def main_kernel(
    NR, NZ, HB,
    panel, trailing,
    factor_out, coupling_out, weights_out, terms_out,
    pan, trl, terms, cacc,
    gram_local, gram_terms, gram_z, gram_zsum, gram_sum, gram_whole,
    prod_terms, prod_sum, prod_whole, work,
    pan_sem, trl_sem, terms_sem,
    right_send, right_recv, left_send, left_recv,
    gram_sems, prod_sems,
):
    me = lax.axis_index("rows")
    z = lax.axis_index("cols")
    owners = min(NR, 16)
    step = NR // owners
    tile = WIDTH // owners
    is_owner = lax.rem(me, step) == 0
    mine = me // step
    half_z = NZ // 2
    events = 2 * half_z - 1
    right, left = lax.rem(z + 1, NZ), lax.rem(z + NZ - 1, NZ)

    pan_copies = [
        pltpu.make_async_copy(panel.at[pl.ds(h * HB, HB)], pan.at[z, h], pan_sem.at[h])
        for h in range(2)
    ]
    for copy in pan_copies:
        copy.start()
    trl_copy = pltpu.make_async_copy(trailing, trl, trl_sem)
    trl_copy.start()

    barrier = pltpu.get_barrier_semaphore()

    def greet_row(k, carry):
        peer = lax.rem(me + k, NR)

        @pl.when(jnp.logical_or(is_owner, lax.rem(peer, step) == 0))
        def _():
            pl.semaphore_signal(barrier, inc=1, device_id=(peer, z), device_id_type=MESH)

        return carry

    def greet_col(k, carry):
        peer = lax.rem(z + k, NZ)

        @pl.when(jnp.logical_or(is_owner, jnp.logical_or(k == 1, k == NZ - 1)))
        def _():
            pl.semaphore_signal(barrier, inc=1, device_id=(me, peer), device_id_type=MESH)

        return carry

    lax.fori_loop(1, NZ, greet_col, 0)
    lax.fori_loop(1, NR, greet_row, 0)

    @pl.when(is_owner)
    def _():
        pl.semaphore_wait(barrier, NR - 1 + NZ - 1)

    @pl.when(jnp.logical_not(is_owner))
    def _():
        pl.semaphore_wait(barrier, owners + 2)

    def ring_copy(event, to_right):
        hop, half = event // 2, event % 2
        if to_right:
            origin = lax.rem(z - hop + NZ, NZ)
            slot, target, send, recv = half, right, right_send, right_recv
        else:
            origin = lax.rem(z + hop, NZ)
            slot, target, send, recv = 1 - half, left, left_send, left_recv
        source = panel.at[pl.ds(slot * HB, HB)] if hop == 0 else pan.at[origin, slot]
        return pltpu.make_async_remote_copy(
            src_ref=source,
            dst_ref=pan.at[origin, slot],
            send_sem=send.at[event],
            recv_sem=recv.at[event],
            device_id=(me, target),
            device_id_type=MESH,
        )

    def arrival(event, from_left):
        hop, half = event // 2 + 1, event % 2
        if from_left:
            origin, slot, recv = lax.rem(z - hop + NZ, NZ), half, right_recv
        else:
            origin, slot, recv = lax.rem(z + hop, NZ), 1 - half, left_recv
        return origin, slot, recv.at[event]

    for event in range(min(2, events)):
        ring_copy(event, True).start()
        ring_copy(event, False).start()

    def rows_of(origin, slot):
        return pl.ds(pl.multiple_of((origin * 2 + slot) * HB, HB), HB)

    def multiply(origin, slot):
        split = split_terms(pan[origin, slot])
        terms[origin, slot] = split
        pltpu.make_async_copy(
            terms.at[origin, slot], terms_out.at[rows_of(origin, slot)], terms_sem
        ).start()
        product = contract_rows(split, split_terms(trl[rows_of(origin, slot), :]))
        cacc[...] += (
            product[:WIDTH, :WIDTH] + product[WIDTH:, :WIDTH] + product[:WIDTH, WIDTH:]
        )

    def handle(event):
        for from_left in (True, False):
            origin, slot, sem = arrival(event, from_left)
            pltpu.make_async_copy(pan.at[origin, slot], pan.at[origin, slot], sem).wait()
            if event + 2 < events:
                ring_copy(event + 2, from_left).start()
        for from_left in (True, False):
            origin, slot, _ = arrival(event, from_left)
            multiply(origin, slot)

    def scatter_start(source, landing, sems):
        def one(index, carry):
            owner = index * step
            part = source.at[pl.ds(pl.multiple_of(index * tile, tile), tile)]

            @pl.when(owner == me)
            def _():
                pltpu.make_async_copy(part, landing.at[me], sems.at[1]).start()

            @pl.when(owner != me)
            def _():
                pltpu.make_async_remote_copy(
                    src_ref=part,
                    dst_ref=landing.at[me],
                    send_sem=sems.at[0],
                    recv_sem=sems.at[1],
                    device_id=(owner, z),
                    device_id_type=MESH,
                ).start()

            return carry

        lax.fori_loop(0, owners, one, 0)

    def total(landing, count):
        value = landing[0]
        for k in range(1, count):
            value = value + landing[k]
        return value

    def scatter_finish(source, landing, sems):
        pltpu.make_async_copy(landing, landing, sems.at[1]).wait()
        return total(landing, NR)

    def spread_start(source, whole, sems):
        part = whole.at[pl.ds(pl.multiple_of(mine * tile, tile), tile)]
        pltpu.make_async_copy(source, part, sems.at[3]).start()

        def one(k, carry):
            pltpu.make_async_remote_copy(
                src_ref=source,
                dst_ref=part,
                send_sem=sems.at[2],
                recv_sem=sems.at[3],
                device_id=(lax.rem(me + k, NR), z),
                device_id_type=MESH,
            ).start()
            return carry

        lax.fori_loop(1, NR, one, 0)

    def sent(ref, sem):
        pltpu.make_async_copy(ref, ref, sem).wait()

    for copy in pan_copies:
        copy.wait()
    gram = None
    for h in range(2):
        own = pan[z, h]
        part = contract_rows(own, own, HIGHEST)
        gram = part if gram is None else gram + part
    gram_local[...] = gram
    scatter_start(gram_local, gram_terms, gram_sems)

    cacc[...] = jnp.zeros_like(cacc)
    trl_copy.wait()
    for h in range(2):
        multiply(z, h)

    @pl.when(is_owner)
    def _():
        gram_zsum[...] = scatter_finish(gram_local, gram_terms, gram_sems)
        pltpu.make_async_copy(gram_zsum, gram_z.at[z], gram_sems.at[5]).start()

        def one(k, carry):
            pltpu.make_async_remote_copy(
                src_ref=gram_zsum,
                dst_ref=gram_z.at[z],
                send_sem=gram_sems.at[4],
                recv_sem=gram_sems.at[5],
                device_id=(me, lax.rem(z + k, NZ)),
                device_id_type=MESH,
            ).start()
            return carry

        lax.fori_loop(1, NZ, one, 0)

    handle(0)

    @pl.when(is_owner)
    def _():
        pltpu.make_async_copy(gram_z, gram_z, gram_sems.at[5]).wait()
        gram_sum[...] = total(gram_z, NZ)
        spread_start(gram_sum, gram_whole, gram_sems)

    handle(1)

    pltpu.make_async_copy(gram_whole, gram_whole, gram_sems.at[3]).wait()
    row_index = lax.broadcasted_iota(jnp.int32, (WIDTH, WIDTH), 0)
    column_index = lax.broadcasted_iota(jnp.int32, (WIDTH, WIDTH), 1)
    work[:, :WIDTH] = gram_whole[...]
    work[:, WIDTH:] = jnp.where(row_index == column_index, 1.0, 0.0).astype(jnp.float32)
    blocks = WIDTH // BLOCK
    middle = max(events - 3, 1)
    handled = 2
    for part in range(middle):
        eliminate(work, blocks * part // middle, blocks * (part + 1) // middle)
        if handled < events - 1:
            handle(handled)
            handled += 1
    upper = jnp.where(row_index <= column_index, work[:, :WIDTH], 0.0)
    diagonal = jnp.sum(
        jnp.where(row_index == column_index, upper, 0.0), axis=1, keepdims=True
    )
    factor_out[...] = upper / jnp.sqrt(diagonal)
    work[:, WIDTH:] = work[:, WIDTH:] / jnp.sqrt(diagonal)
    for event in range(handled, events):
        handle(event)

    scatter_start(cacc, prod_terms, prod_sems)

    @pl.when(is_owner)
    def _():
        prod_sum[...] = scatter_finish(cacc, prod_terms, prod_sems)
        spread_start(prod_sum, prod_whole, prod_sems)

    pltpu.make_async_copy(prod_whole, prod_whole, prod_sems.at[3]).wait()
    inverse_t = work[:, WIDTH:]
    coupling = jnp.dot(
        inverse_t, prod_whole[...], precision=HIGHEST, preferred_element_type=jnp.float32
    )
    coupling_out[...] = coupling
    weights_out[...] = contract_rows(inverse_t, coupling, HIGHEST)

    for event in range(events):
        ring_copy(event, True).wait_send()
        ring_copy(event, False).wait_send()
    sent(terms_out, terms_sem)

    @pl.when(is_owner)
    def _():
        for sems in (gram_sems, prod_sems):
            sent(gram_local.at[: WIDTH - tile], sems.at[0])
            sent(gram_terms.at[: NR - 1], sems.at[2])
        sent(gram_z.at[: NZ - 1], gram_sems.at[4])

    @pl.when(jnp.logical_not(is_owner))
    def _():
        for sems in (gram_sems, prod_sems):
            sent(gram_local, sems.at[0])


def apply_kernel(terms, trailing, weights, factor, coupling, updated, factor_out, coupling_out, pair):
    @pl.when(pl.program_id(0) == 0)
    def _():
        split = split_terms(weights[...])
        pair[:WIDTH, :] = split
        pair[WIDTH:, :] = split
        factor_out[...] = factor[...]
        coupling_out[...] = coupling[...]

    product = jnp.dot(terms[...], pair[...], preferred_element_type=jnp.float32)
    updated[...] = trailing[...] - (product[:, :WIDTH] + product[:, WIDTH:])


def per_device(NR, NZ, panel, trailing):
    HB = panel.shape[0] // 2
    rows = trailing.shape[0]
    owners = min(NR, 16)
    tile = WIDTH // owners
    events = NZ - 1
    f32 = jnp.float32
    square = pltpu.VMEM((WIDTH, WIDTH), f32)
    small = jax.ShapeDtypeStruct((WIDTH, WIDTH), f32)
    in_vmem = pl.BlockSpec(memory_space=pltpu.VMEM)
    anywhere = pl.BlockSpec(memory_space=pl.ANY)
    dma = pltpu.SemaphoreType.DMA
    factor, coupling, weights, terms = pl.pallas_call(
        functools.partial(main_kernel, NR, NZ, HB),
        out_shape=(small, small, small, jax.ShapeDtypeStruct((rows, 2 * WIDTH), jnp.bfloat16)),
        in_specs=[anywhere, anywhere],
        out_specs=(in_vmem, in_vmem, in_vmem, anywhere),
        scratch_shapes=[
            pltpu.VMEM((NZ, 2, HB, WIDTH), f32),
            pltpu.VMEM((rows, WIDTH), f32),
            pltpu.VMEM((NZ, 2, HB, 2 * WIDTH), jnp.bfloat16),
            square,
            square,
            pltpu.VMEM((NR, tile, WIDTH), f32),
            pltpu.VMEM((NZ, tile, WIDTH), f32),
            pltpu.VMEM((tile, WIDTH), f32),
            pltpu.VMEM((tile, WIDTH), f32),
            square,
            pltpu.VMEM((NR, tile, WIDTH), f32),
            pltpu.VMEM((tile, WIDTH), f32),
            square,
            pltpu.VMEM((WIDTH, 2 * WIDTH), f32),
            dma((2,)),
            dma,
            dma,
            dma((events,)),
            dma((events,)),
            dma((events,)),
            dma((events,)),
            dma((6,)),
            dma((4,)),
        ],
        compiler_params=pltpu.CompilerParams(
            collective_id=0, has_side_effects=True, vmem_limit_bytes=VMEM_LIMIT
        ),
        name="gather_factor_couple",
    )(panel, trailing)
    size = min(rows, 1024)
    fixed = pl.BlockSpec((WIDTH, WIDTH), lambda i: (0, 0))
    updated, factor, coupling = pl.pallas_call(
        apply_kernel,
        grid=(rows // size,),
        out_shape=(jax.ShapeDtypeStruct(trailing.shape, f32), small, small),
        in_specs=[
            pl.BlockSpec((size, 2 * WIDTH), lambda i: (i, 0)),
            pl.BlockSpec((size, WIDTH), lambda i: (i, 0)),
            fixed,
            fixed,
            fixed,
        ],
        out_specs=(pl.BlockSpec((size, WIDTH), lambda i: (i, 0)), fixed, fixed),
        scratch_shapes=[pltpu.VMEM((2 * WIDTH, 2 * WIDTH), jnp.bfloat16)],
        compiler_params=pltpu.CompilerParams(vmem_limit_bytes=VMEM_LIMIT),
        name="apply_update",
    )(terms, trailing, weights, factor, coupling)
    return factor, coupling, updated


def solution(mesh):
    return jax.shard_map(
        functools.partial(per_device, mesh.shape["rows"], mesh.shape["cols"]),
        mesh=mesh,
        in_specs=(P(("rows", "cols"), None), P("rows", "cols")),
        out_specs=(P(), P(None, "cols"), P("rows", "cols")),
        check_vma=False,
    )
```

```python
import functools

import jax
import jax.numpy as jnp
from jax import lax
from jax.experimental import pallas as pl
from jax.experimental.pallas import tpu as pltpu
from jax.sharding import PartitionSpec as P

MESH = pl.DeviceIdType.MESH
HIGHEST = lax.Precision.HIGHEST
WIDTH = 128
BLOCK = 8
MAIN_VMEM = 52 * 1024 * 1024
APPLY_VMEM = 16 * 1024 * 1024


def split_terms(value):
    high = value.astype(jnp.bfloat16)
    low = (value - high.astype(jnp.float32)).astype(jnp.bfloat16)
    return jnp.concatenate([high, low], axis=1)


def contract_rows(left, right, precision=None):
    return lax.dot_general(
        left,
        right,
        (((0,), (0,)), ((), ())),
        precision=precision,
        preferred_element_type=jnp.float32,
    )


def eliminate(work, first, last):
    lane = lax.broadcasted_iota(jnp.int32, (BLOCK, WIDTH), 1)
    sub = lax.broadcasted_iota(jnp.int32, (BLOCK, WIDTH), 0)

    def one_block(index, carry):
        start = pl.multiple_of(index * BLOCK, BLOCK)
        rows = work[pl.ds(start, BLOCK), :]
        gram_part = rows[:, :WIDTH]
        columns = []
        for a in range(BLOCK):
            picked = jnp.where(lane == start + a, gram_part, 0.0)
            column = jnp.sum(picked, axis=1, keepdims=True)
            columns.append(jnp.broadcast_to(column, (BLOCK, WIDTH)))
        scale = jnp.zeros((BLOCK, WIDTH), jnp.float32)
        for a in range(BLOCK):
            inverse = 1.0 / jnp.broadcast_to(columns[a][a : a + 1, :], (BLOCK, WIDTH))
            scale = jnp.where(sub == a, inverse, scale)
            factor = jnp.where(sub > a, columns[a] * inverse, 0.0)
            for d in range(a + 1, BLOCK):
                pivot_row = jnp.broadcast_to(columns[d][a : a + 1, :], (BLOCK, WIDTH))
                columns[d] = columns[d] - factor * pivot_row
            pivot_row = jnp.broadcast_to(rows[a : a + 1, :], (BLOCK, 2 * WIDTH))
            rows = rows - jnp.concatenate([factor, factor], axis=1) * pivot_row
        work[pl.ds(start, BLOCK), :] = rows
        lower = jnp.where(lane >= start + BLOCK, rows[:, :WIDTH] * scale, 0.0)
        work[...] = work[...] - contract_rows(lower, rows, HIGHEST)
        return carry

    lax.fori_loop(first, last, one_block, 0)


def main_kernel(
    NR, NZ, HB,
    panel, trailing,
    factor_out, coupling_out, weights_out, terms, trl,
    pan, cacc,
    gram_local, gram_terms, gram_z, gram_zsum, gram_sum, gram_whole,
    prod_terms, prod_sum, prod_whole, work,
    pan_sem, trl_sem,
    right_send, right_recv, left_send, left_recv,
    gram_sems, prod_sems,
):
    me = lax.axis_index("rows")
    z = lax.axis_index("cols")
    owners = min(NR, 16)
    step = NR // owners
    tile = WIDTH // owners
    is_owner = lax.rem(me, step) == 0
    mine = me // step
    half_z = NZ // 2
    events = 2 * half_z - 1
    right, left = lax.rem(z + 1, NZ), lax.rem(z + NZ - 1, NZ)

    pan_copies = [
        pltpu.make_async_copy(panel.at[pl.ds(h * HB, HB)], pan.at[z, h], pan_sem.at[h])
        for h in range(2)
    ]
    for copy in pan_copies:
        copy.start()
    trl_copy = pltpu.make_async_copy(trailing, trl, trl_sem)
    trl_copy.start()

    barrier = pltpu.get_barrier_semaphore()

    def greet_row(k, carry):
        peer = lax.rem(me + k, NR)

        @pl.when(jnp.logical_or(is_owner, lax.rem(peer, step) == 0))
        def _():
            pl.semaphore_signal(barrier, inc=1, device_id=(peer, z), device_id_type=MESH)

        return carry

    def greet_col(k, carry):
        peer = lax.rem(z + k, NZ)

        @pl.when(jnp.logical_or(is_owner, jnp.logical_or(k == 1, k == NZ - 1)))
        def _():
            pl.semaphore_signal(barrier, inc=1, device_id=(me, peer), device_id_type=MESH)

        return carry

    lax.fori_loop(1, NZ, greet_col, 0)
    lax.fori_loop(1, NR, greet_row, 0)

    @pl.when(is_owner)
    def _():
        pl.semaphore_wait(barrier, NR - 1 + NZ - 1)

    @pl.when(jnp.logical_not(is_owner))
    def _():
        pl.semaphore_wait(barrier, owners + 2)

    def ring_copy(event, to_right):
        hop, half = event // 2, event % 2
        if to_right:
            origin = lax.rem(z - hop + NZ, NZ)
            slot, target, send, recv = half, right, right_send, right_recv
        else:
            origin = lax.rem(z + hop, NZ)
            slot, target, send, recv = 1 - half, left, left_send, left_recv
        source = panel.at[pl.ds(slot * HB, HB)] if hop == 0 else pan.at[origin, slot]
        return pltpu.make_async_remote_copy(
            src_ref=source,
            dst_ref=pan.at[origin, slot],
            send_sem=send.at[event],
            recv_sem=recv.at[event],
            device_id=(me, target),
            device_id_type=MESH,
        )

    def arrival(event, from_left):
        hop, half = event // 2 + 1, event % 2
        if from_left:
            origin, slot, recv = lax.rem(z - hop + NZ, NZ), half, right_recv
        else:
            origin, slot, recv = lax.rem(z + hop, NZ), 1 - half, left_recv
        return origin, slot, recv.at[event]

    for event in range(min(2, events)):
        ring_copy(event, True).start()
        ring_copy(event, False).start()

    def rows_of(origin, slot):
        return pl.ds(pl.multiple_of((origin * 2 + slot) * HB, HB), HB)

    def multiply(origin, slot):
        split = split_terms(pan[origin, slot])
        terms[rows_of(origin, slot), :] = split
        product = contract_rows(split, split_terms(trl[rows_of(origin, slot), :]))
        cacc[...] += (
            product[:WIDTH, :WIDTH] + product[WIDTH:, :WIDTH] + product[:WIDTH, WIDTH:]
        )

    def handle(event):
        for from_left in (True, False):
            origin, slot, sem = arrival(event, from_left)
            pltpu.make_async_copy(pan.at[origin, slot], pan.at[origin, slot], sem).wait()
            if event + 2 < events:
                ring_copy(event + 2, from_left).start()
        for from_left in (True, False):
            origin, slot, _ = arrival(event, from_left)
            multiply(origin, slot)

    def scatter_start(source, landing, sems):
        def one(index, carry):
            owner = index * step
            part = source.at[pl.ds(pl.multiple_of(index * tile, tile), tile)]

            @pl.when(owner == me)
            def _():
                pltpu.make_async_copy(part, landing.at[me], sems.at[1]).start()

            @pl.when(owner != me)
            def _():
                pltpu.make_async_remote_copy(
                    src_ref=part,
                    dst_ref=landing.at[me],
                    send_sem=sems.at[0],
                    recv_sem=sems.at[1],
                    device_id=(owner, z),
                    device_id_type=MESH,
                ).start()

            return carry

        lax.fori_loop(0, owners, one, 0)

    def total(landing, count):
        value = landing[0]
        for k in range(1, count):
            value = value + landing[k]
        return value

    def scatter_finish(source, landing, sems):
        pltpu.make_async_copy(landing, landing, sems.at[1]).wait()
        return total(landing, NR)

    def spread_start(source, whole, sems):
        part = whole.at[pl.ds(pl.multiple_of(mine * tile, tile), tile)]
        pltpu.make_async_copy(source, part, sems.at[3]).start()

        def one(k, carry):
            pltpu.make_async_remote_copy(
                src_ref=source,
                dst_ref=part,
                send_sem=sems.at[2],
                recv_sem=sems.at[3],
                device_id=(lax.rem(me + k, NR), z),
                device_id_type=MESH,
            ).start()
            return carry

        lax.fori_loop(1, NR, one, 0)

    def sent(ref, sem):
        pltpu.make_async_copy(ref, ref, sem).wait()

    for copy in pan_copies:
        copy.wait()
    gram = None
    for h in range(2):
        own = pan[z, h]
        part = contract_rows(own, own, HIGHEST)
        gram = part if gram is None else gram + part
    gram_local[...] = gram
    scatter_start(gram_local, gram_terms, gram_sems)

    cacc[...] = jnp.zeros_like(cacc)
    trl_copy.wait()
    for h in range(2):
        multiply(z, h)

    @pl.when(is_owner)
    def _():
        gram_zsum[...] = scatter_finish(gram_local, gram_terms, gram_sems)
        pltpu.make_async_copy(gram_zsum, gram_z.at[z], gram_sems.at[5]).start()

        def one(k, carry):
            pltpu.make_async_remote_copy(
                src_ref=gram_zsum,
                dst_ref=gram_z.at[z],
                send_sem=gram_sems.at[4],
                recv_sem=gram_sems.at[5],
                device_id=(me, lax.rem(z + k, NZ)),
                device_id_type=MESH,
            ).start()
            return carry

        lax.fori_loop(1, NZ, one, 0)

    handle(0)

    @pl.when(is_owner)
    def _():
        pltpu.make_async_copy(gram_z, gram_z, gram_sems.at[5]).wait()
        gram_sum[...] = total(gram_z, NZ)
        spread_start(gram_sum, gram_whole, gram_sems)

    handle(1)

    pltpu.make_async_copy(gram_whole, gram_whole, gram_sems.at[3]).wait()
    row_index = lax.broadcasted_iota(jnp.int32, (WIDTH, WIDTH), 0)
    column_index = lax.broadcasted_iota(jnp.int32, (WIDTH, WIDTH), 1)
    work[:, :WIDTH] = gram_whole[...]
    work[:, WIDTH:] = jnp.where(row_index == column_index, 1.0, 0.0).astype(jnp.float32)
    blocks = WIDTH // BLOCK
    middle = max(events - 3, 1)
    handled = 2
    for part in range(middle):
        eliminate(work, blocks * part // middle, blocks * (part + 1) // middle)
        if handled < events - 1:
            handle(handled)
            handled += 1
    upper = jnp.where(row_index <= column_index, work[:, :WIDTH], 0.0)
    diagonal = jnp.sum(
        jnp.where(row_index == column_index, upper, 0.0), axis=1, keepdims=True
    )
    factor_out[...] = upper / jnp.sqrt(diagonal)
    work[:, WIDTH:] = work[:, WIDTH:] / jnp.sqrt(diagonal)
    for event in range(handled, events):
        handle(event)

    scatter_start(cacc, prod_terms, prod_sems)

    @pl.when(is_owner)
    def _():
        prod_sum[...] = scatter_finish(cacc, prod_terms, prod_sems)
        spread_start(prod_sum, prod_whole, prod_sems)

    pltpu.make_async_copy(prod_whole, prod_whole, prod_sems.at[3]).wait()
    inverse_t = work[:, WIDTH:]
    coupling = jnp.dot(
        inverse_t, prod_whole[...], precision=HIGHEST, preferred_element_type=jnp.float32
    )
    coupling_out[...] = coupling
    weights_out[...] = contract_rows(inverse_t, coupling, HIGHEST)

    for event in range(events):
        ring_copy(event, True).wait_send()
        ring_copy(event, False).wait_send()

    @pl.when(is_owner)
    def _():
        for sems in (gram_sems, prod_sems):
            sent(gram_local.at[: WIDTH - tile], sems.at[0])
            sent(gram_terms.at[: NR - 1], sems.at[2])
        sent(gram_z.at[: NZ - 1], gram_sems.at[4])

    @pl.when(jnp.logical_not(is_owner))
    def _():
        for sems in (gram_sems, prod_sems):
            sent(gram_local, sems.at[0])


def apply_kernel(size, terms, trailing, weights, factor, coupling, updated, factor_out, coupling_out, pair, held, sem):
    split = split_terms(weights[...])
    pair[:WIDTH, :] = split
    pair[WIDTH:, :] = split
    factor_out[...] = factor[...]
    coupling_out[...] = coupling[...]
    for start in range(0, held.shape[0], size):
        rows = pl.ds(start, size)
        product = jnp.dot(terms[rows, :], pair[...], preferred_element_type=jnp.float32)
        held[rows, :] = trailing[rows, :] - (product[:, :WIDTH] + product[:, WIDTH:])
        pltpu.make_async_copy(held.at[rows], updated.at[rows], sem).start()
    pltpu.make_async_copy(held, updated, sem).wait()


def per_device(NR, NZ, panel, trailing):
    HB = panel.shape[0] // 2
    rows = trailing.shape[0]
    owners = min(NR, 16)
    tile = WIDTH // owners
    events = NZ - 1
    f32 = jnp.float32
    square = pltpu.VMEM((WIDTH, WIDTH), f32)
    small = jax.ShapeDtypeStruct((WIDTH, WIDTH), f32)
    kept_terms = pltpu.VMEM((rows, 2 * WIDTH), jnp.bfloat16)
    kept_rows = pltpu.VMEM((rows, WIDTH), f32)
    in_vmem = pl.BlockSpec(memory_space=pltpu.VMEM)
    anywhere = pl.BlockSpec(memory_space=pl.ANY)
    dma = pltpu.SemaphoreType.DMA
    factor, coupling, weights, terms, kept = pl.pallas_call(
        functools.partial(main_kernel, NR, NZ, HB),
        out_shape=(square, square, square, kept_terms, kept_rows),
        in_specs=[anywhere, anywhere],
        out_specs=(in_vmem,) * 5,
        scratch_shapes=[
            pltpu.VMEM((NZ, 2, HB, WIDTH), f32),
            square,
            square,
            pltpu.VMEM((NR, tile, WIDTH), f32),
            pltpu.VMEM((NZ, tile, WIDTH), f32),
            pltpu.VMEM((tile, WIDTH), f32),
            pltpu.VMEM((tile, WIDTH), f32),
            square,
            pltpu.VMEM((NR, tile, WIDTH), f32),
            pltpu.VMEM((tile, WIDTH), f32),
            square,
            pltpu.VMEM((WIDTH, 2 * WIDTH), f32),
            dma((2,)),
            dma,
            dma((events,)),
            dma((events,)),
            dma((events,)),
            dma((events,)),
            dma((6,)),
            dma((4,)),
        ],
        compiler_params=pltpu.CompilerParams(
            collective_id=0, has_side_effects=True, vmem_limit_bytes=MAIN_VMEM
        ),
        name="gather_factor_couple",
    )(panel, trailing)
    updated, factor, coupling = pl.pallas_call(
        functools.partial(apply_kernel, min(rows, 1024)),
        out_shape=(jax.ShapeDtypeStruct(trailing.shape, f32), small, small),
        in_specs=[in_vmem] * 5,
        out_specs=(anywhere, in_vmem, in_vmem),
        scratch_shapes=[
            pltpu.VMEM((2 * WIDTH, 2 * WIDTH), jnp.bfloat16),
            pltpu.VMEM((rows, WIDTH), f32),
            dma,
        ],
        compiler_params=pltpu.CompilerParams(vmem_limit_bytes=APPLY_VMEM),
        name="apply_update",
    )(terms, kept, weights, factor, coupling)
    return factor, coupling, updated


def solution(mesh):
    return jax.shard_map(
        functools.partial(per_device, mesh.shape["rows"], mesh.shape["cols"]),
        mesh=mesh,
        in_specs=(P(("rows", "cols"), None), P("rows", "cols")),
        out_specs=(P(), P(None, "cols"), P("rows", "cols")),
        check_vma=False,
    )
```

```python
import functools

import jax
import jax.numpy as jnp
from jax import lax
from jax.experimental import pallas as pl
from jax.experimental.pallas import tpu as pltpu
from jax.sharding import PartitionSpec as P

MESH = pl.DeviceIdType.MESH
HIGHEST = lax.Precision.HIGHEST
WIDTH = 128
BLOCK = 8
MAIN_VMEM = 52 * 1024 * 1024
APPLY_VMEM = 16 * 1024 * 1024


def split_terms(value):
    high = value.astype(jnp.bfloat16)
    low = (value - high.astype(jnp.float32)).astype(jnp.bfloat16)
    return jnp.concatenate([high, low], axis=1)


def contract_rows(left, right, precision=None):
    return lax.dot_general(
        left,
        right,
        (((0,), (0,)), ((), ())),
        precision=precision,
        preferred_element_type=jnp.float32,
    )


def eliminate(work, first, last):
    lane = lax.broadcasted_iota(jnp.int32, (BLOCK, WIDTH), 1)
    sub = lax.broadcasted_iota(jnp.int32, (BLOCK, WIDTH), 0)

    def one_block(index, carry):
        start = pl.multiple_of(index * BLOCK, BLOCK)
        rows = work[pl.ds(start, BLOCK), :]
        gram_part = rows[:, :WIDTH]
        columns = []
        for a in range(BLOCK):
            picked = jnp.where(lane == start + a, gram_part, 0.0)
            column = jnp.sum(picked, axis=1, keepdims=True)
            columns.append(jnp.broadcast_to(column, (BLOCK, WIDTH)))
        scale = jnp.zeros((BLOCK, WIDTH), jnp.float32)
        for a in range(BLOCK):
            inverse = 1.0 / jnp.broadcast_to(columns[a][a : a + 1, :], (BLOCK, WIDTH))
            scale = jnp.where(sub == a, inverse, scale)
            factor = jnp.where(sub > a, columns[a] * inverse, 0.0)
            for d in range(a + 1, BLOCK):
                pivot_row = jnp.broadcast_to(columns[d][a : a + 1, :], (BLOCK, WIDTH))
                columns[d] = columns[d] - factor * pivot_row
            pivot_row = jnp.broadcast_to(rows[a : a + 1, :], (BLOCK, 2 * WIDTH))
            rows = rows - jnp.concatenate([factor, factor], axis=1) * pivot_row
        work[pl.ds(start, BLOCK), :] = rows
        lower = jnp.where(lane >= start + BLOCK, rows[:, :WIDTH] * scale, 0.0)
        work[...] = work[...] - contract_rows(lower, rows, HIGHEST)
        return carry

    lax.fori_loop(first, last, one_block, 0)


def plane_side(NR):
    side = 1
    while side * side * 2 < NR:
        side *= 2
    return side


def near_rounds(NR, NZ):
    return max(2 * (plane_side(NR) // 2) + 1, NZ // 2) - 1


def main_kernel(
    NR, NZ, HB,
    panel, trailing,
    factor_out, coupling_out, weights_out, terms, trl,
    pan, cacc,
    gram_local, gram_terms, gram_z, gram_zsum, gram_sum, gram_whole,
    line_terms, half_sum, cross_terms, prod_whole, work,
    pan_sem, trl_sem,
    right_send, right_recv, left_send, left_recv,
    gram_sems, prod_sems, near_sems,
):
    me = lax.axis_index("rows")
    z = lax.axis_index("cols")
    owners = min(NR, 16)
    step = NR // owners
    tile = WIDTH // owners
    is_owner = lax.rem(me, step) == 0
    mine = me // step
    half_z = NZ // 2
    events = 2 * half_z - 1
    right, left = lax.rem(z + 1, NZ), lax.rem(z + NZ - 1, NZ)

    pan_copies = [
        pltpu.make_async_copy(panel.at[pl.ds(h * HB, HB)], pan.at[z, h], pan_sem.at[h])
        for h in range(2)
    ]
    for copy in pan_copies:
        copy.start()
    trl_copy = pltpu.make_async_copy(trailing, trl, trl_sem)
    trl_copy.start()

    side, core, chip = plane_side(NR), lax.rem(me, 2), me // 2
    x, y = lax.rem(chip, side), chip // side

    def device(row, column, which):
        return (row * side + column) * 2 + which

    neighbours = [(me, right), (me, left), (device(y, x, 1 - core), z)]
    if side > 1:
        for move in (1, side - 1):
            neighbours.append((device(y, lax.rem(x + move, side), core), z))
            neighbours.append((device(lax.rem(y + move, side), x, core), z))

    def greet(sem):
        for neighbour in neighbours:
            pl.semaphore_signal(sem, inc=1, device_id=neighbour, device_id_type=MESH)

    def meet(k):
        if k < near_rounds(NR, NZ):
            pl.semaphore_wait(near_sems.at[k], len(neighbours))
            if k + 1 < near_rounds(NR, NZ):
                greet(near_sems.at[k + 1])

    barrier = pltpu.get_barrier_semaphore()
    greet(barrier)
    pl.semaphore_wait(barrier, len(neighbours))

    def ring_copy(event, to_right):
        hop, half = event // 2, event % 2
        if to_right:
            origin = lax.rem(z - hop + NZ, NZ)
            slot, target, send, recv = half, right, right_send, right_recv
        else:
            origin = lax.rem(z + hop, NZ)
            slot, target, send, recv = 1 - half, left, left_send, left_recv
        source = panel.at[pl.ds(slot * HB, HB)] if hop == 0 else pan.at[origin, slot]
        return pltpu.make_async_remote_copy(
            src_ref=source,
            dst_ref=pan.at[origin, slot],
            send_sem=send.at[event],
            recv_sem=recv.at[event],
            device_id=(me, target),
            device_id_type=MESH,
        )

    def arrival(event, from_left):
        hop, half = event // 2 + 1, event % 2
        if from_left:
            origin, slot, recv = lax.rem(z - hop + NZ, NZ), half, right_recv
        else:
            origin, slot, recv = lax.rem(z + hop, NZ), 1 - half, left_recv
        return origin, slot, recv.at[event]

    for event in range(min(2, events)):
        ring_copy(event, True).start()
        ring_copy(event, False).start()

    if near_rounds(NR, NZ):
        greet(near_sems.at[0])

    def rows_of(origin, slot):
        return pl.ds(pl.multiple_of((origin * 2 + slot) * HB, HB), HB)

    def multiply(origin, slot):
        split = split_terms(pan[origin, slot])
        terms[rows_of(origin, slot), :] = split
        product = contract_rows(split, split_terms(trl[rows_of(origin, slot), :]))
        cacc[...] += (
            product[:WIDTH, :WIDTH] + product[WIDTH:, :WIDTH] + product[:WIDTH, WIDTH:]
        )

    def handle(event):
        if event >= events:
            return
        for from_left in (True, False):
            origin, slot, sem = arrival(event, from_left)
            pltpu.make_async_copy(pan.at[origin, slot], pan.at[origin, slot], sem).wait()
            if event + 2 < events:
                ring_copy(event + 2, from_left).start()
        for from_left in (True, False):
            origin, slot, _ = arrival(event, from_left)
            multiply(origin, slot)

    def scatter_start(source, landing, sems):
        def one(index, carry):
            owner = index * step
            part = source.at[pl.ds(pl.multiple_of(index * tile, tile), tile)]

            @pl.when(owner == me)
            def _():
                pltpu.make_async_copy(part, landing.at[me], sems.at[1]).start()

            @pl.when(owner != me)
            def _():
                pltpu.make_async_remote_copy(
                    src_ref=part,
                    dst_ref=landing.at[me],
                    send_sem=sems.at[0],
                    recv_sem=sems.at[1],
                    device_id=(owner, z),
                    device_id_type=MESH,
                ).start()

            return carry

        lax.fori_loop(0, owners, one, 0)

    def total(landing, count):
        value = landing[0]
        for k in range(1, count):
            value = value + landing[k]
        return value

    def scatter_finish(source, landing, sems):
        pltpu.make_async_copy(landing, landing, sems.at[1]).wait()
        return total(landing, NR)

    def spread_start(source, whole, sems):
        part = whole.at[pl.ds(pl.multiple_of(mine * tile, tile), tile)]
        pltpu.make_async_copy(source, part, sems.at[3]).start()

        def one(k, carry):
            pltpu.make_async_remote_copy(
                src_ref=source,
                dst_ref=part,
                send_sem=sems.at[2],
                recv_sem=sems.at[3],
                device_id=(lax.rem(me + k, NR), z),
                device_id_type=MESH,
            ).start()
            return carry

        lax.fori_loop(1, NR, one, 0)

    def sent(ref, sem):
        pltpu.make_async_copy(ref, ref, sem).wait()

    for copy in pan_copies:
        copy.wait()
    gram = None
    for h in range(2):
        own = pan[z, h]
        part = contract_rows(own, own, HIGHEST)
        gram = part if gram is None else gram + part
    gram_local[...] = gram
    cacc[...] = jnp.zeros_like(cacc)
    meet(0)
    trl_copy.wait()
    for h in range(2):
        multiply(z, h)
        meet(1 + h)
    handle(0)
    meet(3)
    scatter_start(gram_local, gram_terms, gram_sems)
    handle(1)

    @pl.when(is_owner)
    def _():
        gram_zsum[...] = scatter_finish(gram_local, gram_terms, gram_sems)
        pltpu.make_async_copy(gram_zsum, gram_z.at[z], gram_sems.at[5]).start()

        def one(k, carry):
            pltpu.make_async_remote_copy(
                src_ref=gram_zsum,
                dst_ref=gram_z.at[z],
                send_sem=gram_sems.at[4],
                recv_sem=gram_sems.at[5],
                device_id=(me, lax.rem(z + k, NZ)),
                device_id_type=MESH,
            ).start()
            return carry

        lax.fori_loop(1, NZ, one, 0)

    handle(2)

    @pl.when(is_owner)
    def _():
        pltpu.make_async_copy(gram_z, gram_z, gram_sems.at[5]).wait()
        gram_sum[...] = total(gram_z, NZ)
        spread_start(gram_sum, gram_whole, gram_sems)

    handle(3)
    pltpu.make_async_copy(gram_whole, gram_whole, gram_sems.at[3]).wait()
    row_index = lax.broadcasted_iota(jnp.int32, (WIDTH, WIDTH), 0)
    column_index = lax.broadcasted_iota(jnp.int32, (WIDTH, WIDTH), 1)
    work[:, :WIDTH] = gram_whole[...]
    work[:, WIDTH:] = jnp.where(row_index == column_index, 1.0, 0.0).astype(jnp.float32)
    blocks = WIDTH // BLOCK
    eliminate(work, 0, blocks * 5 // 8)
    handle(4)
    eliminate(work, blocks * 5 // 8, blocks)
    upper = jnp.where(row_index <= column_index, work[:, :WIDTH], 0.0)
    diagonal = jnp.sum(
        jnp.where(row_index == column_index, upper, 0.0), axis=1, keepdims=True
    )
    factor_out[...] = upper / jnp.sqrt(diagonal)
    work[:, WIDTH:] = work[:, WIDTH:] / jnp.sqrt(diagonal)
    for event in range(5, events):
        handle(event)

    moves = sorted(range(side), key=lambda move: -min(move, side - move))
    deep = WIDTH // 2

    def deliver(source, target, sems, peer):
        @pl.when(peer == me)
        def _():
            pltpu.make_async_copy(source, target, sems.at[1]).start()

        @pl.when(peer != me)
        def _():
            pltpu.make_async_remote_copy(
                src_ref=source,
                dst_ref=target,
                send_sem=sems.at[0],
                recv_sem=sems.at[1],
                device_id=(peer, z),
                device_id_type=MESH,
            ).start()

    first, second = prod_sems.at[0], prod_sems.at[1]
    for move in moves:
        along_x, along_y = lax.rem(x + move, side), lax.rem(y + move, side)
        deliver(cacc.at[:deep], line_terms.at[x * 2 + core], first, device(y, along_x, 0))
        deliver(cacc.at[deep:], line_terms.at[y * 2 + core], first, device(along_y, x, 1))
    sent(line_terms, first.at[1])
    half_sum[...] = total(line_terms, 2 * side)
    for move in moves:
        along_x, along_y = lax.rem(x + move, side), lax.rem(y + move, side)
        for which in range(2):

            @pl.when(core == 0)
            def _():
                deliver(half_sum, cross_terms.at[0, y], second, device(along_y, x, which))

            @pl.when(core == 1)
            def _():
                deliver(half_sum, cross_terms.at[1, x], second, device(y, along_x, which))

    sent(cross_terms, second.at[1])
    prod_whole[:deep, :] = total(cross_terms.at[0], side)
    prod_whole[deep:, :] = total(cross_terms.at[1], side)
    inverse_t = work[:, WIDTH:]
    coupling = jnp.dot(
        inverse_t, prod_whole[...], precision=HIGHEST, preferred_element_type=jnp.float32
    )
    coupling_out[...] = coupling
    weights_out[...] = contract_rows(inverse_t, coupling, HIGHEST)

    for event in range(events):
        ring_copy(event, True).wait_send()
        ring_copy(event, False).wait_send()

    for sems in (first, second):
        sent(line_terms.at[: 2 * side - 1], sems.at[0])

    @pl.when(is_owner)
    def _():
        sent(gram_local.at[: WIDTH - tile], gram_sems.at[0])
        sent(gram_terms.at[: NR - 1], gram_sems.at[2])
        sent(gram_z.at[: NZ - 1], gram_sems.at[4])

    @pl.when(jnp.logical_not(is_owner))
    def _():
        sent(gram_local, gram_sems.at[0])


def apply_kernel(size, terms, trailing, weights, factor, coupling, updated, factor_out, coupling_out, pair, held, sem, small_sem):
    factor_copy = pltpu.make_async_copy(factor, factor_out, small_sem.at[0])
    coupling_copy = pltpu.make_async_copy(coupling, coupling_out, small_sem.at[1])
    factor_copy.start()
    coupling_copy.start()
    split = split_terms(weights[...])
    pair[:WIDTH, :] = split
    pair[WIDTH:, :] = split
    for start in range(0, held.shape[0], size):
        rows = pl.ds(start, size)
        product = jnp.dot(terms[rows, :], pair[...], preferred_element_type=jnp.float32)
        held[rows, :] = trailing[rows, :] - (product[:, :WIDTH] + product[:, WIDTH:])
        pltpu.make_async_copy(held.at[rows], updated.at[rows], sem).start()
    pltpu.make_async_copy(held, updated, sem).wait()
    factor_copy.wait()
    coupling_copy.wait()


def per_device(NR, NZ, panel, trailing):
    HB = panel.shape[0] // 2
    rows = trailing.shape[0]
    owners = min(NR, 16)
    tile = WIDTH // owners
    events = NZ - 1
    side = plane_side(NR)
    f32 = jnp.float32
    square = pltpu.VMEM((WIDTH, WIDTH), f32)
    small = jax.ShapeDtypeStruct((WIDTH, WIDTH), f32)
    kept_terms = pltpu.VMEM((rows, 2 * WIDTH), jnp.bfloat16)
    kept_rows = pltpu.VMEM((rows, WIDTH), f32)
    in_vmem = pl.BlockSpec(memory_space=pltpu.VMEM)
    anywhere = pl.BlockSpec(memory_space=pl.ANY)
    dma = pltpu.SemaphoreType.DMA
    factor, coupling, weights, terms, kept = pl.pallas_call(
        functools.partial(main_kernel, NR, NZ, HB),
        out_shape=(square, square, square, kept_terms, kept_rows),
        in_specs=[anywhere, anywhere],
        out_specs=(in_vmem,) * 5,
        scratch_shapes=[
            pltpu.VMEM((NZ, 2, HB, WIDTH), f32),
            square,
            square,
            pltpu.VMEM((NR, tile, WIDTH), f32),
            pltpu.VMEM((NZ, tile, WIDTH), f32),
            pltpu.VMEM((tile, WIDTH), f32),
            pltpu.VMEM((tile, WIDTH), f32),
            square,
            pltpu.VMEM((2 * side, WIDTH // 2, WIDTH), f32),
            pltpu.VMEM((WIDTH // 2, WIDTH), f32),
            pltpu.VMEM((2, side, WIDTH // 2, WIDTH), f32),
            square,
            pltpu.VMEM((WIDTH, 2 * WIDTH), f32),
            dma((2,)),
            dma,
            dma((events,)),
            dma((events,)),
            dma((events,)),
            dma((events,)),
            dma((6,)),
            dma((2, 2)),
            pltpu.SemaphoreType.REGULAR((max(near_rounds(NR, NZ), 1),)),
        ],
        compiler_params=pltpu.CompilerParams(
            collective_id=0, has_side_effects=True, vmem_limit_bytes=MAIN_VMEM
        ),
        name="gather_factor_couple",
    )(panel, trailing)
    updated, factor, coupling = pl.pallas_call(
        functools.partial(apply_kernel, min(rows, 1024)),
        out_shape=(jax.ShapeDtypeStruct(trailing.shape, f32), small, small),
        in_specs=[in_vmem] * 5,
        out_specs=(anywhere,) * 3,
        scratch_shapes=[
            pltpu.VMEM((2 * WIDTH, 2 * WIDTH), jnp.bfloat16),
            pltpu.VMEM((rows, WIDTH), f32),
            dma,
            dma((2,)),
        ],
        compiler_params=pltpu.CompilerParams(vmem_limit_bytes=APPLY_VMEM),
        name="apply_update",
    )(terms, kept, weights, factor, coupling)
    return factor, coupling, updated


def solution(mesh):
    return jax.shard_map(
        functools.partial(per_device, mesh.shape["rows"], mesh.shape["cols"]),
        mesh=mesh,
        in_specs=(P(("rows", "cols"), None), P("rows", "cols")),
        out_specs=(P(), P(None, "cols"), P("rows", "cols")),
        check_vma=False,
    )
```

```python
import functools

import jax
import jax.numpy as jnp
from jax import lax
from jax.experimental import pallas as pl
from jax.experimental.pallas import tpu as pltpu
from jax.sharding import PartitionSpec as P

MESH = pl.DeviceIdType.MESH
HIGHEST = lax.Precision.HIGHEST
WIDTH = 128
BLOCK = 8
PARTS = 4
MAIN_VMEM = 52 * 1024 * 1024
APPLY_VMEM = 16 * 1024 * 1024


def split_terms(value):
    high = value.astype(jnp.bfloat16)
    low = (value - high.astype(jnp.float32)).astype(jnp.bfloat16)
    return jnp.concatenate([high, low], axis=1)


def contract_rows(left, right, precision=None):
    return lax.dot_general(
        left,
        right,
        (((0,), (0,)), ((), ())),
        precision=precision,
        preferred_element_type=jnp.float32,
    )


def eliminate(work, first, last):
    lane = lax.broadcasted_iota(jnp.int32, (BLOCK, WIDTH), 1)
    sub = lax.broadcasted_iota(jnp.int32, (BLOCK, WIDTH), 0)

    def one_block(index, carry):
        start = pl.multiple_of(index * BLOCK, BLOCK)
        rows = work[pl.ds(start, BLOCK), :]
        gram_part = rows[:, :WIDTH]
        columns = []
        for a in range(BLOCK):
            picked = jnp.where(lane == start + a, gram_part, 0.0)
            column = jnp.sum(picked, axis=1, keepdims=True)
            columns.append(jnp.broadcast_to(column, (BLOCK, WIDTH)))
        scale = jnp.zeros((BLOCK, WIDTH), jnp.float32)
        for a in range(BLOCK):
            inverse = 1.0 / jnp.broadcast_to(columns[a][a : a + 1, :], (BLOCK, WIDTH))
            scale = jnp.where(sub == a, inverse, scale)
            factor = jnp.where(sub > a, columns[a] * inverse, 0.0)
            for d in range(a + 1, BLOCK):
                pivot_row = jnp.broadcast_to(columns[d][a : a + 1, :], (BLOCK, WIDTH))
                columns[d] = columns[d] - factor * pivot_row
            pivot_row = jnp.broadcast_to(rows[a : a + 1, :], (BLOCK, 2 * WIDTH))
            rows = rows - jnp.concatenate([factor, factor], axis=1) * pivot_row
        work[pl.ds(start, BLOCK), :] = rows
        lower = jnp.where(lane >= start + BLOCK, rows[:, :WIDTH] * scale, 0.0)
        work[...] = work[...] - contract_rows(lower, rows, HIGHEST)
        return carry

    lax.fori_loop(first, last, one_block, 0)


def plane_side(NR):
    side = 1
    while side * side * 2 < NR:
        side *= 2
    return side


def ring_events(NZ):
    return PARTS * (NZ // 2 - 1) + PARTS // 2


def near_rounds(NR):
    return 2 * (plane_side(NR) // 2)


def main_kernel(
    NR, NZ, HB,
    panel, trailing,
    factor_out, coupling_out, weights_out, terms, trl,
    pan, cacc,
    gram_local, gram_terms, gram_z, gram_zsum, gram_sum, gram_whole,
    line_terms, half_sum, cross_terms, prod_whole, work,
    pan_sem, trl_sem,
    right_send, right_recv, left_send, left_recv,
    gram_sems, prod_sems, near_sems, line_sems,
):
    me = lax.axis_index("rows")
    z = lax.axis_index("cols")
    owners = min(NR, 16)
    step = NR // owners
    tile = WIDTH // owners
    is_owner = lax.rem(me, step) == 0
    mine = me // step
    events = ring_events(NZ)
    right, left = lax.rem(z + 1, NZ), lax.rem(z + NZ - 1, NZ)

    side, core, chip = plane_side(NR), lax.rem(me, 2), me // 2
    x, y = lax.rem(chip, side), chip // side

    def device(row, column, which):
        return (row * side + column) * 2 + which

    line = [(me, right), (me, left)]
    neighbours = [(device(y, x, 1 - core), z)]
    if side > 1:
        for move in (1, side - 1):
            neighbours.append((device(y, lax.rem(x + move, side), core), z))
            neighbours.append((device(lax.rem(y + move, side), x, core), z))

    def greet(sem, devices):
        for other in devices:
            pl.semaphore_signal(sem, inc=1, device_id=other, device_id_type=MESH)

    def meet(k):
        if k < near_rounds(NR):
            pl.semaphore_wait(near_sems.at[k], len(neighbours))
            if k + 1 < near_rounds(NR):
                greet(near_sems.at[k + 1], neighbours)

    def meet_line(k):
        if NZ >= 4 * (k + 1):
            pl.semaphore_wait(line_sems.at[k], 2)
        if k == 0 and NZ >= 8:
            for move in (2, NZ - 2):
                greet(line_sems.at[1], [(me, lax.rem(z + move, NZ))])

    barrier = pltpu.get_barrier_semaphore()
    greet(barrier, line + neighbours)
    pan_copies = [
        pltpu.make_async_copy(panel.at[pl.ds(h * HB, HB)], pan.at[z, h], pan_sem.at[h])
        for h in range(PARTS)
    ]
    for copy in pan_copies:
        copy.start()
    trl_copy = pltpu.make_async_copy(trailing, trl, trl_sem)
    trl_copy.start()
    pl.semaphore_wait(barrier, len(line + neighbours))

    def ring_copy(event, to_right):
        hop, part = event // PARTS, event % PARTS
        if to_right:
            origin = lax.rem(z - hop + NZ, NZ)
            slot, target, send, recv = part, right, right_send, right_recv
        else:
            origin = lax.rem(z + hop, NZ)
            slot, target, send, recv = PARTS - 1 - part, left, left_send, left_recv
        source = panel.at[pl.ds(slot * HB, HB)] if hop == 0 else pan.at[origin, slot]
        return pltpu.make_async_remote_copy(
            src_ref=source,
            dst_ref=pan.at[origin, slot],
            send_sem=send.at[event],
            recv_sem=recv.at[event],
            device_id=(me, target),
            device_id_type=MESH,
        )

    def arrival(event, from_left):
        hop, part = event // PARTS + 1, event % PARTS
        if from_left:
            origin, slot, recv = lax.rem(z - hop + NZ, NZ), part, right_recv
        else:
            origin, slot, recv = lax.rem(z + hop, NZ), PARTS - 1 - part, left_recv
        return origin, slot, recv.at[event]

    def send(event):
        if event < events:
            ring_copy(event, True).start()
            ring_copy(event, False).start()

    if NZ >= 4:
        greet(line_sems.at[0], line)
    for event in range(PARTS // 2):
        send(event)
    if near_rounds(NR):
        greet(near_sems.at[0], neighbours)

    def rows_of(origin, slot):
        return pl.ds(pl.multiple_of((origin * PARTS + slot) * HB, HB), HB)

    def multiply(origin, slot):
        split = split_terms(pan[origin, slot])
        terms[rows_of(origin, slot), :] = split
        product = contract_rows(split, split_terms(trl[rows_of(origin, slot), :]))
        cacc[...] += (
            product[:WIDTH, :WIDTH] + product[WIDTH:, :WIDTH] + product[:WIDTH, WIDTH:]
        )

    def handle(event, forward=True):
        if event >= events:
            return
        for from_left in (True, False):
            origin, slot, sem = arrival(event, from_left)
            pltpu.make_async_copy(pan.at[origin, slot], pan.at[origin, slot], sem).wait()
        if forward:
            send(event + PARTS)
        for from_left in (True, False):
            origin, slot, _ = arrival(event, from_left)
            multiply(origin, slot)

    def scatter_start(source, landing, sems):
        def one(index, carry):
            owner = index * step
            part = source.at[pl.ds(pl.multiple_of(index * tile, tile), tile)]

            @pl.when(owner == me)
            def _():
                pltpu.make_async_copy(part, landing.at[me], sems.at[1]).start()

            @pl.when(owner != me)
            def _():
                pltpu.make_async_remote_copy(
                    src_ref=part,
                    dst_ref=landing.at[me],
                    send_sem=sems.at[0],
                    recv_sem=sems.at[1],
                    device_id=(owner, z),
                    device_id_type=MESH,
                ).start()

            return carry

        lax.fori_loop(0, owners, one, 0)

    def total(landing, count):
        value = landing[0]
        for k in range(1, count):
            value = value + landing[k]
        return value

    def scatter_finish(source, landing, sems):
        pltpu.make_async_copy(landing, landing, sems.at[1]).wait()
        return total(landing, NR)

    def spread_start(source, whole, sems):
        part = whole.at[pl.ds(pl.multiple_of(mine * tile, tile), tile)]
        pltpu.make_async_copy(source, part, sems.at[3]).start()

        def one(k, carry):
            pltpu.make_async_remote_copy(
                src_ref=source,
                dst_ref=part,
                send_sem=sems.at[2],
                recv_sem=sems.at[3],
                device_id=(lax.rem(me + k, NR), z),
                device_id_type=MESH,
            ).start()
            return carry

        lax.fori_loop(1, NR, one, 0)

    def sent(ref, sem):
        pltpu.make_async_copy(ref, ref, sem).wait()

    for copy in pan_copies:
        copy.wait()
    gram = None
    for h in range(PARTS):
        own = pan[z, h]
        part = contract_rows(own, own, HIGHEST)
        gram = part if gram is None else gram + part
    gram_local[...] = gram
    cacc[...] = jnp.zeros_like(cacc)
    meet(0)
    meet_line(0)
    for event in range(PARTS // 2, PARTS):
        send(event)
    trl_copy.wait()
    for h in range(PARTS):
        multiply(z, h)
    meet(1)
    meet(2)
    handle(0, forward=False)
    meet(3)
    scatter_start(gram_local, gram_terms, gram_sems)
    handle(1, forward=False)
    handle(2, forward=False)
    send(PARTS)
    meet_line(1)

    @pl.when(is_owner)
    def _():
        gram_zsum[...] = scatter_finish(gram_local, gram_terms, gram_sems)
        pltpu.make_async_copy(gram_zsum, gram_z.at[z], gram_sems.at[5]).start()

        def one(k, carry):
            pltpu.make_async_remote_copy(
                src_ref=gram_zsum,
                dst_ref=gram_z.at[z],
                send_sem=gram_sems.at[4],
                recv_sem=gram_sems.at[5],
                device_id=(me, lax.rem(z + k, NZ)),
                device_id_type=MESH,
            ).start()
            return carry

        lax.fori_loop(1, NZ, one, 0)

    send(PARTS + 1)
    send(PARTS + 2)
    handle(3)
    handle(4)
    handle(5)

    @pl.when(is_owner)
    def _():
        pltpu.make_async_copy(gram_z, gram_z, gram_sems.at[5]).wait()
        gram_sum[...] = total(gram_z, NZ)
        spread_start(gram_sum, gram_whole, gram_sems)

    handle(6)
    handle(7)
    pltpu.make_async_copy(gram_whole, gram_whole, gram_sems.at[3]).wait()
    row_index = lax.broadcasted_iota(jnp.int32, (WIDTH, WIDTH), 0)
    column_index = lax.broadcasted_iota(jnp.int32, (WIDTH, WIDTH), 1)
    work[:, :WIDTH] = gram_whole[...]
    work[:, WIDTH:] = jnp.where(row_index == column_index, 1.0, 0.0).astype(jnp.float32)
    blocks = WIDTH // BLOCK
    for part in range(4):
        eliminate(work, blocks * part // 4, blocks * (part + 1) // 4)
        if part < 3:
            handle(8 + part)
    upper = jnp.where(row_index <= column_index, work[:, :WIDTH], 0.0)
    diagonal = jnp.sum(
        jnp.where(row_index == column_index, upper, 0.0), axis=1, keepdims=True
    )
    factor_out[...] = upper / jnp.sqrt(diagonal)
    work[:, WIDTH:] = work[:, WIDTH:] / jnp.sqrt(diagonal)
    for event in range(11, events):
        handle(event)

    moves = sorted(range(side), key=lambda move: -min(move, side - move))
    deep = WIDTH // 2

    def deliver(source, target, sems, peer):
        @pl.when(peer == me)
        def _():
            pltpu.make_async_copy(source, target, sems.at[1]).start()

        @pl.when(peer != me)
        def _():
            pltpu.make_async_remote_copy(
                src_ref=source,
                dst_ref=target,
                send_sem=sems.at[0],
                recv_sem=sems.at[1],
                device_id=(peer, z),
                device_id_type=MESH,
            ).start()

    first, second = prod_sems.at[0], prod_sems.at[1]
    for move in moves:
        along_x, along_y = lax.rem(x + move, side), lax.rem(y + move, side)
        deliver(cacc.at[:deep], line_terms.at[x * 2 + core], first, device(y, along_x, 0))
        deliver(cacc.at[deep:], line_terms.at[y * 2 + core], first, device(along_y, x, 1))
    sent(line_terms, first.at[1])
    half_sum[...] = total(line_terms, 2 * side)
    for move in moves:
        along_x, along_y = lax.rem(x + move, side), lax.rem(y + move, side)
        for which in range(2):

            @pl.when(core == 0)
            def _():
                deliver(half_sum, cross_terms.at[0, y], second, device(along_y, x, which))

            @pl.when(core == 1)
            def _():
                deliver(half_sum, cross_terms.at[1, x], second, device(y, along_x, which))

    sent(cross_terms, second.at[1])
    prod_whole[:deep, :] = total(cross_terms.at[0], side)
    prod_whole[deep:, :] = total(cross_terms.at[1], side)
    inverse_t = work[:, WIDTH:]
    coupling = jnp.dot(
        inverse_t, prod_whole[...], precision=HIGHEST, preferred_element_type=jnp.float32
    )
    coupling_out[...] = coupling
    weights_out[...] = contract_rows(inverse_t, coupling, HIGHEST)

    for event in range(events):
        ring_copy(event, True).wait_send()
        ring_copy(event, False).wait_send()

    for sems in (first, second):
        sent(line_terms.at[: 2 * side - 1], sems.at[0])

    @pl.when(is_owner)
    def _():
        sent(gram_local.at[: WIDTH - tile], gram_sems.at[0])
        sent(gram_terms.at[: NR - 1], gram_sems.at[2])
        sent(gram_z.at[: NZ - 1], gram_sems.at[4])

    @pl.when(jnp.logical_not(is_owner))
    def _():
        sent(gram_local, gram_sems.at[0])


def apply_kernel(size, terms, trailing, weights, factor, coupling, updated, factor_out, coupling_out, pair, held, sem, small_sem):
    factor_copy = pltpu.make_async_copy(factor, factor_out, small_sem.at[0])
    coupling_copy = pltpu.make_async_copy(coupling, coupling_out, small_sem.at[1])
    factor_copy.start()
    coupling_copy.start()
    split = split_terms(weights[...])
    pair[:WIDTH, :] = split
    pair[WIDTH:, :] = split
    for start in range(0, held.shape[0], size):
        rows = pl.ds(start, size)
        product = jnp.dot(terms[rows, :], pair[...], preferred_element_type=jnp.float32)
        held[rows, :] = trailing[rows, :] - (product[:, :WIDTH] + product[:, WIDTH:])
        pltpu.make_async_copy(held.at[rows], updated.at[rows], sem).start()
    pltpu.make_async_copy(held, updated, sem).wait()
    factor_copy.wait()
    coupling_copy.wait()


def per_device(NR, NZ, panel, trailing):
    HB = panel.shape[0] // PARTS
    rows = trailing.shape[0]
    owners = min(NR, 16)
    tile = WIDTH // owners
    events = ring_events(NZ)
    side = plane_side(NR)
    f32 = jnp.float32
    square = pltpu.VMEM((WIDTH, WIDTH), f32)
    small = jax.ShapeDtypeStruct((WIDTH, WIDTH), f32)
    kept_terms = pltpu.VMEM((rows, 2 * WIDTH), jnp.bfloat16)
    kept_rows = pltpu.VMEM((rows, WIDTH), f32)
    in_vmem = pl.BlockSpec(memory_space=pltpu.VMEM)
    anywhere = pl.BlockSpec(memory_space=pl.ANY)
    dma = pltpu.SemaphoreType.DMA
    factor, coupling, weights, terms, kept = pl.pallas_call(
        functools.partial(main_kernel, NR, NZ, HB),
        out_shape=(square, square, square, kept_terms, kept_rows),
        in_specs=[anywhere, anywhere],
        out_specs=(in_vmem,) * 5,
        scratch_shapes=[
            pltpu.VMEM((NZ, PARTS, HB, WIDTH), f32),
            square,
            square,
            pltpu.VMEM((NR, tile, WIDTH), f32),
            pltpu.VMEM((NZ, tile, WIDTH), f32),
            pltpu.VMEM((tile, WIDTH), f32),
            pltpu.VMEM((tile, WIDTH), f32),
            square,
            pltpu.VMEM((2 * side, WIDTH // 2, WIDTH), f32),
            pltpu.VMEM((WIDTH // 2, WIDTH), f32),
            pltpu.VMEM((2, side, WIDTH // 2, WIDTH), f32),
            square,
            pltpu.VMEM((WIDTH, 2 * WIDTH), f32),
            dma((PARTS,)),
            dma,
            dma((events,)),
            dma((events,)),
            dma((events,)),
            dma((events,)),
            dma((6,)),
            dma((2, 2)),
            pltpu.SemaphoreType.REGULAR((max(near_rounds(NR), 1),)),
            pltpu.SemaphoreType.REGULAR((2,)),
        ],
        compiler_params=pltpu.CompilerParams(
            collective_id=0, has_side_effects=True, vmem_limit_bytes=MAIN_VMEM
        ),
        name="gather_factor_couple",
    )(panel, trailing)
    updated, factor, coupling = pl.pallas_call(
        functools.partial(apply_kernel, min(rows, 1024)),
        out_shape=(jax.ShapeDtypeStruct(trailing.shape, f32), small, small),
        in_specs=[in_vmem] * 5,
        out_specs=(anywhere,) * 3,
        scratch_shapes=[
            pltpu.VMEM((2 * WIDTH, 2 * WIDTH), jnp.bfloat16),
            pltpu.VMEM((rows, WIDTH), f32),
            dma,
            dma((2,)),
        ],
        compiler_params=pltpu.CompilerParams(vmem_limit_bytes=APPLY_VMEM),
        name="apply_update",
    )(terms, kept, weights, factor, coupling)
    return factor, coupling, updated


def solution(mesh):
    return jax.shard_map(
        functools.partial(per_device, mesh.shape["rows"], mesh.shape["cols"]),
        mesh=mesh,
        in_specs=(P(("rows", "cols"), None), P("rows", "cols")),
        out_specs=(P(), P(None, "cols"), P("rows", "cols")),
        check_vma=False,
    )
```

```python
import functools

import jax
import jax.numpy as jnp
from jax import lax
from jax.experimental import pallas as pl
from jax.experimental.pallas import tpu as pltpu
from jax.sharding import PartitionSpec as P

MESH = pl.DeviceIdType.MESH
HIGHEST = lax.Precision.HIGHEST
WIDTH = 128
BLOCK = 8
PARTS = 4
MAIN_VMEM = 52 * 1024 * 1024
APPLY_VMEM = 16 * 1024 * 1024


def split_terms(value):
    high = value.astype(jnp.bfloat16)
    low = (value - high.astype(jnp.float32)).astype(jnp.bfloat16)
    return jnp.concatenate([high, low], axis=1)


def contract_rows(left, right, precision=None):
    return lax.dot_general(
        left,
        right,
        (((0,), (0,)), ((), ())),
        precision=precision,
        preferred_element_type=jnp.float32,
    )


def eliminate(work, first, count):
    lane = lax.broadcasted_iota(jnp.int32, (BLOCK, WIDTH), 1)
    sub = lax.broadcasted_iota(jnp.int32, (BLOCK, WIDTH), 0)

    def one_block(index, carry):
        start = pl.multiple_of((first + index) * BLOCK, BLOCK)
        rows = work[pl.ds(start, BLOCK), :]
        gram_part = rows[:, :WIDTH]
        columns = []
        for a in range(BLOCK):
            picked = jnp.where(lane == start + a, gram_part, 0.0)
            column = jnp.sum(picked, axis=1, keepdims=True)
            columns.append(jnp.broadcast_to(column, (BLOCK, WIDTH)))
        scale = jnp.zeros((BLOCK, WIDTH), jnp.float32)
        for a in range(BLOCK):
            inverse = 1.0 / jnp.broadcast_to(columns[a][a : a + 1, :], (BLOCK, WIDTH))
            scale = jnp.where(sub == a, inverse, scale)
            factor = jnp.where(sub > a, columns[a] * inverse, 0.0)
            for d in range(a + 1, BLOCK):
                pivot_row = jnp.broadcast_to(columns[d][a : a + 1, :], (BLOCK, WIDTH))
                columns[d] = columns[d] - factor * pivot_row
            pivot_row = jnp.broadcast_to(rows[a : a + 1, :], (BLOCK, 2 * WIDTH))
            rows = rows - jnp.concatenate([factor, factor], axis=1) * pivot_row
        work[pl.ds(start, BLOCK), :] = rows
        lower = jnp.where(lane >= start + BLOCK, rows[:, :WIDTH] * scale, 0.0)
        work[...] = work[...] - contract_rows(lower, rows, HIGHEST)
        return carry

    lax.fori_loop(0, count, one_block, 0)


def plane_side(NR):
    side = 1
    while side * side * 2 < NR:
        side *= 2
    return side


def ring_events(NZ):
    return PARTS * (NZ // 2 - 1) + PARTS // 2


def near_rounds(NR):
    return 2 * (plane_side(NR) // 2)


def main_kernel(
    NR, NZ, HB,
    panel, trailing,
    factor_out, coupling_out, weights_out, terms, trl,
    pan, cacc,
    gram_local, gram_terms, gram_z, gram_zsum, gram_sum, gram_whole,
    line_terms, half_sum, cross_terms, prod_whole, work,
    pan_sem, trl_sem,
    right_send, right_recv, left_send, left_recv,
    gram_sems, prod_sems, near_sems, line_sems,
):
    me = lax.axis_index("rows")
    z = lax.axis_index("cols")
    owners = min(NR, 16)
    step = NR // owners
    tile = WIDTH // owners
    is_owner = lax.rem(me, step) == 0
    mine = me // step
    events = ring_events(NZ)
    right, left = lax.rem(z + 1, NZ), lax.rem(z + NZ - 1, NZ)

    side, core, chip = plane_side(NR), lax.rem(me, 2), me // 2
    x, y = lax.rem(chip, side), chip // side

    def device(row, column, which):
        return (row * side + column) * 2 + which

    line = [(me, right), (me, left)]
    neighbours = [(device(y, x, 1 - core), z)]
    if side > 1:
        for move in (1, side - 1):
            neighbours.append((device(y, lax.rem(x + move, side), core), z))
            neighbours.append((device(lax.rem(y + move, side), x, core), z))

    def greet(sem, devices):
        for other in devices:
            pl.semaphore_signal(sem, inc=1, device_id=other, device_id_type=MESH)

    def meet(k):
        if k < near_rounds(NR):
            pl.semaphore_wait(near_sems.at[k], len(neighbours))
            if k + 1 < near_rounds(NR):
                greet(near_sems.at[k + 1], neighbours)

    def meet_line(k):
        if NZ >= 4 * (k + 1):
            pl.semaphore_wait(line_sems.at[k], 2)
        if k == 0 and NZ >= 8:
            for move in (2, NZ - 2):
                greet(line_sems.at[1], [(me, lax.rem(z + move, NZ))])

    barrier = pltpu.get_barrier_semaphore()
    greet(barrier, line + neighbours)
    pan_copies = [
        pltpu.make_async_copy(panel.at[pl.ds(h * HB, HB)], pan.at[z, h], pan_sem.at[h])
        for h in range(PARTS)
    ]
    for copy in pan_copies:
        copy.start()
    trl_copy = pltpu.make_async_copy(trailing, trl, trl_sem)
    trl_copy.start()
    pl.semaphore_wait(barrier, len(line + neighbours))

    def place(event, back, to_right):
        part = event % PARTS
        if to_right:
            return lax.rem(z - event // PARTS - back + NZ, NZ), part
        return lax.rem(z + event // PARTS + back, NZ), PARTS - 1 - part

    def send(event, own=False):
        for to_right in (True, False):
            origin, slot = place(event, 0, to_right)
            here = pan.at[origin, slot]
            pltpu.make_async_remote_copy(
                src_ref=panel.at[pl.ds(slot * HB, HB)] if own else here,
                dst_ref=here,
                send_sem=(right_send if to_right else left_send).at[event],
                recv_sem=(right_recv if to_right else left_recv).at[event],
                device_id=(me, right if to_right else left),
                device_id_type=MESH,
            ).start()

    def sent(ref, sem):
        pltpu.make_async_copy(ref, ref, sem).wait()

    if NZ >= 4:
        greet(line_sems.at[0], line)
    for event in range(PARTS // 2):
        send(event, own=True)
    if near_rounds(NR):
        greet(near_sems.at[0], neighbours)

    def rows_of(origin, slot):
        return pl.ds(pl.multiple_of((origin * PARTS + slot) * HB, HB), HB)

    def multiply(origin, slot):
        split = split_terms(pan[origin, slot])
        terms[rows_of(origin, slot), :] = split
        product = contract_rows(split, split_terms(trl[rows_of(origin, slot), :]))
        cacc[...] += (
            product[:WIDTH, :WIDTH] + product[WIDTH:, :WIDTH] + product[:WIDTH, WIDTH:]
        )

    def handle(event, forward):
        for from_left in (True, False):
            origin, slot = place(event, 1, from_left)
            sent(pan.at[origin, slot], (right_recv if from_left else left_recv).at[event])
        if forward:

            @pl.when(event + PARTS < events)
            def _():
                send(event + PARTS)

        for from_left in (True, False):
            multiply(*place(event, 1, from_left))

    def handle_range(first, last, forward=True):
        def one(event, carry):
            handle(event, forward)
            return carry

        if first < min(last, events):
            lax.fori_loop(first, min(last, events), one, 0)

    def forward_range(first, last):
        for event in range(first, min(last, events)):
            send(event)

    def scatter_start(source, landing, sems):
        def one(index, carry):
            owner = index * step
            part = source.at[pl.ds(pl.multiple_of(index * tile, tile), tile)]

            @pl.when(owner == me)
            def _():
                pltpu.make_async_copy(part, landing.at[me], sems.at[1]).start()

            @pl.when(owner != me)
            def _():
                pltpu.make_async_remote_copy(
                    src_ref=part,
                    dst_ref=landing.at[me],
                    send_sem=sems.at[0],
                    recv_sem=sems.at[1],
                    device_id=(owner, z),
                    device_id_type=MESH,
                ).start()

            return carry

        lax.fori_loop(0, owners, one, 0)

    def total(landing, count):
        value = landing[0]
        for k in range(1, count):
            value = value + landing[k]
        return value

    def scatter_finish(source, landing, sems):
        pltpu.make_async_copy(landing, landing, sems.at[1]).wait()
        return total(landing, NR)

    def spread_start(source, whole, sems):
        part = whole.at[pl.ds(pl.multiple_of(mine * tile, tile), tile)]
        pltpu.make_async_copy(source, part, sems.at[3]).start()

        def one(k, carry):
            pltpu.make_async_remote_copy(
                src_ref=source,
                dst_ref=part,
                send_sem=sems.at[2],
                recv_sem=sems.at[3],
                device_id=(lax.rem(me + k, NR), z),
                device_id_type=MESH,
            ).start()
            return carry

        lax.fori_loop(1, NR, one, 0)

    for copy in pan_copies:
        copy.wait()
    gram = None
    for h in range(PARTS):
        own = pan[z, h]
        part = contract_rows(own, own, HIGHEST)
        gram = part if gram is None else gram + part
    gram_local[...] = gram
    cacc[...] = jnp.zeros_like(cacc)
    meet(0)
    meet_line(0)
    for event in range(PARTS // 2, min(PARTS, events)):
        send(event, own=True)
    trl_copy.wait()
    for h in range(PARTS):
        multiply(z, h)
    meet(1)
    meet(2)
    handle_range(0, 1, forward=False)
    meet(3)
    scatter_start(gram_local, gram_terms, gram_sems)
    handle_range(1, 2, forward=False)
    forward_range(PARTS, PARTS + 1)
    handle_range(2, 3, forward=False)
    meet_line(1)

    @pl.when(is_owner)
    def _():
        gram_zsum[...] = scatter_finish(gram_local, gram_terms, gram_sems)
        pltpu.make_async_copy(gram_zsum, gram_z.at[z], gram_sems.at[5]).start()

        def one(k, carry):
            pltpu.make_async_remote_copy(
                src_ref=gram_zsum,
                dst_ref=gram_z.at[z],
                send_sem=gram_sems.at[4],
                recv_sem=gram_sems.at[5],
                device_id=(me, lax.rem(z + k, NZ)),
                device_id_type=MESH,
            ).start()
            return carry

        lax.fori_loop(1, NZ, one, 0)

    forward_range(PARTS + 1, PARTS + 3)
    handle_range(3, 6)

    @pl.when(is_owner)
    def _():
        pltpu.make_async_copy(gram_z, gram_z, gram_sems.at[5]).wait()
        gram_sum[...] = total(gram_z, NZ)
        spread_start(gram_sum, gram_whole, gram_sems)

    handle_range(6, 8)
    pltpu.make_async_copy(gram_whole, gram_whole, gram_sems.at[3]).wait()
    row_index = lax.broadcasted_iota(jnp.int32, (WIDTH, WIDTH), 0)
    column_index = lax.broadcasted_iota(jnp.int32, (WIDTH, WIDTH), 1)
    work[:, :WIDTH] = gram_whole[...]
    work[:, WIDTH:] = jnp.where(row_index == column_index, 1.0, 0.0).astype(jnp.float32)
    blocks = WIDTH // BLOCK

    def eliminate_part(part, carry):
        eliminate(work, part * (blocks // 4), blocks // 4)

        @pl.when(part + 8 < events)
        def _():
            handle(part + 8, True)

        return carry

    lax.fori_loop(0, 4, eliminate_part, 0)
    upper = jnp.where(row_index <= column_index, work[:, :WIDTH], 0.0)
    diagonal = jnp.sum(
        jnp.where(row_index == column_index, upper, 0.0), axis=1, keepdims=True
    )
    factor_out[...] = upper / jnp.sqrt(diagonal)
    work[:, WIDTH:] = work[:, WIDTH:] / jnp.sqrt(diagonal)
    handle_range(12, events, forward=False)

    moves = sorted(range(side), key=lambda move: -min(move, side - move))
    deep = WIDTH // 2

    def deliver(source, target, sems, peer):
        @pl.when(peer == me)
        def _():
            pltpu.make_async_copy(source, target, sems.at[1]).start()

        @pl.when(peer != me)
        def _():
            pltpu.make_async_remote_copy(
                src_ref=source,
                dst_ref=target,
                send_sem=sems.at[0],
                recv_sem=sems.at[1],
                device_id=(peer, z),
                device_id_type=MESH,
            ).start()

    first, second = prod_sems.at[0], prod_sems.at[1]
    for move in moves:
        along_x, along_y = lax.rem(x + move, side), lax.rem(y + move, side)
        deliver(cacc.at[:deep], line_terms.at[x * 2 + core], first, device(y, along_x, 0))
        deliver(cacc.at[deep:], line_terms.at[y * 2 + core], first, device(along_y, x, 1))

    def ring_sent(event, carry):
        sent(pan.at[0, 0], right_send.at[event])
        sent(pan.at[0, 0], left_send.at[event])
        return carry

    lax.fori_loop(0, events, ring_sent, 0)

    @pl.when(is_owner)
    def _():
        sent(gram_local.at[: WIDTH - tile], gram_sems.at[0])
        sent(gram_terms.at[: NR - 1], gram_sems.at[2])
        sent(gram_z.at[: NZ - 1], gram_sems.at[4])

    @pl.when(jnp.logical_not(is_owner))
    def _():
        sent(gram_local, gram_sems.at[0])

    sent(line_terms, first.at[1])
    half_sum[...] = total(line_terms, 2 * side)
    for move in moves:
        along_x, along_y = lax.rem(x + move, side), lax.rem(y + move, side)
        for which in range(2):

            @pl.when(core == 0)
            def _():
                deliver(half_sum, cross_terms.at[0, y], second, device(along_y, x, which))

            @pl.when(core == 1)
            def _():
                deliver(half_sum, cross_terms.at[1, x], second, device(y, along_x, which))

    sent(cross_terms, second.at[1])
    prod_whole[:deep, :] = total(cross_terms.at[0], side)
    prod_whole[deep:, :] = total(cross_terms.at[1], side)
    inverse_t = work[:, WIDTH:]
    coupling = jnp.dot(
        inverse_t, prod_whole[...], precision=HIGHEST, preferred_element_type=jnp.float32
    )
    coupling_out[...] = coupling
    weights_out[...] = contract_rows(inverse_t, coupling, HIGHEST)

    for sems in (first, second):
        sent(line_terms.at[: 2 * side - 1], sems.at[0])


def apply_kernel(size, terms, trailing, weights, factor, coupling, updated, factor_out, coupling_out, pair, held, sem, small_sem):
    factor_copy = pltpu.make_async_copy(factor, factor_out, small_sem.at[0])
    coupling_copy = pltpu.make_async_copy(coupling, coupling_out, small_sem.at[1])
    factor_copy.start()
    coupling_copy.start()
    split = split_terms(weights[...])
    pair[:WIDTH, :] = split
    pair[WIDTH:, :] = split
    for start in range(0, held.shape[0], size):
        rows = pl.ds(start, size)
        product = jnp.dot(terms[rows, :], pair[...], preferred_element_type=jnp.float32)
        held[rows, :] = trailing[rows, :] - (product[:, :WIDTH] + product[:, WIDTH:])
        pltpu.make_async_copy(held.at[rows], updated.at[rows], sem).start()
    pltpu.make_async_copy(held, updated, sem).wait()
    factor_copy.wait()
    coupling_copy.wait()


def per_device(NR, NZ, panel, trailing):
    HB = panel.shape[0] // PARTS
    rows = trailing.shape[0]
    owners = min(NR, 16)
    tile = WIDTH // owners
    events = ring_events(NZ)
    side = plane_side(NR)
    f32 = jnp.float32
    square = pltpu.VMEM((WIDTH, WIDTH), f32)
    small = jax.ShapeDtypeStruct((WIDTH, WIDTH), f32)
    kept_terms = pltpu.VMEM((rows, 2 * WIDTH), jnp.bfloat16)
    kept_rows = pltpu.VMEM((rows, WIDTH), f32)
    in_vmem = pl.BlockSpec(memory_space=pltpu.VMEM)
    anywhere = pl.BlockSpec(memory_space=pl.ANY)
    dma = pltpu.SemaphoreType.DMA
    factor, coupling, weights, terms, kept = pl.pallas_call(
        functools.partial(main_kernel, NR, NZ, HB),
        out_shape=(square, square, square, kept_terms, kept_rows),
        in_specs=[anywhere, anywhere],
        out_specs=(in_vmem,) * 5,
        scratch_shapes=[
            pltpu.VMEM((NZ, PARTS, HB, WIDTH), f32),
            square,
            square,
            pltpu.VMEM((NR, tile, WIDTH), f32),
            pltpu.VMEM((NZ, tile, WIDTH), f32),
            pltpu.VMEM((tile, WIDTH), f32),
            pltpu.VMEM((tile, WIDTH), f32),
            square,
            pltpu.VMEM((2 * side, WIDTH // 2, WIDTH), f32),
            pltpu.VMEM((WIDTH // 2, WIDTH), f32),
            pltpu.VMEM((2, side, WIDTH // 2, WIDTH), f32),
            square,
            pltpu.VMEM((WIDTH, 2 * WIDTH), f32),
            dma((PARTS,)),
            dma,
            dma((events,)),
            dma((events,)),
            dma((events,)),
            dma((events,)),
            dma((6,)),
            dma((2, 2)),
            pltpu.SemaphoreType.REGULAR((max(near_rounds(NR), 1),)),
            pltpu.SemaphoreType.REGULAR((2,)),
        ],
        compiler_params=pltpu.CompilerParams(
            collective_id=0, has_side_effects=True, vmem_limit_bytes=MAIN_VMEM
        ),
        name="gather_factor_couple",
    )(panel, trailing)
    updated, factor, coupling = pl.pallas_call(
        functools.partial(apply_kernel, min(rows, 128)),
        out_shape=(jax.ShapeDtypeStruct(trailing.shape, f32), small, small),
        in_specs=[in_vmem] * 5,
        out_specs=(anywhere,) * 3,
        scratch_shapes=[
            pltpu.VMEM((2 * WIDTH, 2 * WIDTH), jnp.bfloat16),
            pltpu.VMEM((rows, WIDTH), f32),
            dma,
            dma((2,)),
        ],
        compiler_params=pltpu.CompilerParams(vmem_limit_bytes=APPLY_VMEM),
        name="apply_update",
    )(terms, kept, weights, factor, coupling)
    return factor, coupling, updated


def solution(mesh):
    return jax.shard_map(
        functools.partial(per_device, mesh.shape["rows"], mesh.shape["cols"]),
        mesh=mesh,
        in_specs=(P(("rows", "cols"), None), P("rows", "cols")),
        out_specs=(P(), P(None, "cols"), P("rows", "cols")),
        check_vma=False,
    )
```

```python
import functools

import jax
import jax.numpy as jnp
from jax import lax
from jax.experimental import pallas as pl
from jax.experimental.pallas import tpu as pltpu
from jax.sharding import PartitionSpec as P

MESH = pl.DeviceIdType.MESH
HIGHEST = lax.Precision.HIGHEST
WIDTH = 128
BLOCK = 8
PARTS = 4
MAIN_VMEM = 52 * 1024 * 1024
APPLY_VMEM = 16 * 1024 * 1024


def split_terms(value):
    high = value.astype(jnp.bfloat16)
    low = (value - high.astype(jnp.float32)).astype(jnp.bfloat16)
    return jnp.concatenate([high, low], axis=1)


def twice(pair, value):
    split = split_terms(value)
    pair[:WIDTH, :] = split
    pair[WIDTH:, :] = split


def contract_rows(left, right, precision=None):
    return lax.dot_general(
        left,
        right,
        (((0,), (0,)), ((), ())),
        precision=precision,
        preferred_element_type=jnp.float32,
    )


def eliminate(work, first, count):
    lane = lax.broadcasted_iota(jnp.int32, (BLOCK, WIDTH), 1)
    sub = lax.broadcasted_iota(jnp.int32, (BLOCK, WIDTH), 0)

    def one_block(index, carry):
        start = pl.multiple_of((first + index) * BLOCK, BLOCK)
        rows = work[pl.ds(start, BLOCK), :]
        gram_part = rows[:, :WIDTH]
        columns = []
        for a in range(BLOCK):
            picked = jnp.where(lane == start + a, gram_part, 0.0)
            column = jnp.sum(picked, axis=1, keepdims=True)
            columns.append(jnp.broadcast_to(column, (BLOCK, WIDTH)))
        scale = jnp.zeros((BLOCK, WIDTH), jnp.float32)
        for a in range(BLOCK):
            inverse = 1.0 / jnp.broadcast_to(columns[a][a : a + 1, :], (BLOCK, WIDTH))
            scale = jnp.where(sub == a, inverse, scale)
            factor = jnp.where(sub > a, columns[a] * inverse, 0.0)
            for d in range(a + 1, BLOCK):
                pivot_row = jnp.broadcast_to(columns[d][a : a + 1, :], (BLOCK, WIDTH))
                columns[d] = columns[d] - factor * pivot_row
            pivot_row = jnp.broadcast_to(rows[a : a + 1, :], (BLOCK, 2 * WIDTH))
            rows = rows - jnp.concatenate([factor, factor], axis=1) * pivot_row
        work[pl.ds(start, BLOCK), :] = rows
        lower = jnp.where(lane >= start + BLOCK, rows[:, :WIDTH] * scale, 0.0)
        work[...] = work[...] - contract_rows(lower, rows, HIGHEST)
        return carry

    lax.fori_loop(0, count, one_block, 0)


def plane_side(NR):
    side = 1
    while side * side * 2 < NR:
        side *= 2
    return side


def ring_events(NZ):
    return PARTS * (NZ // 2 - 1) + PARTS // 2


def near_rounds(NR):
    return 2 * (plane_side(NR) // 2)


def main_kernel(
    NR, NZ, HB,
    panel, trailing,
    factor_out, coupling_out, terms, trl,
    pan, cacc,
    gram_local, gram_terms, gram_z, gram_zsum, gram_sum, gram_whole,
    line_terms, half_sum, cross_terms, prod_whole, work, pair,
    pan_sem, trl_sem,
    right_send, right_recv, left_send, left_recv,
    gram_sems, prod_sems, near_sems, line_sems,
):
    me = lax.axis_index("rows")
    z = lax.axis_index("cols")
    owners = min(NR, 16)
    step = NR // owners
    tile = WIDTH // owners
    is_owner = lax.rem(me, step) == 0
    mine = me // step
    events = ring_events(NZ)
    right, left = lax.rem(z + 1, NZ), lax.rem(z + NZ - 1, NZ)

    side, core, chip = plane_side(NR), lax.rem(me, 2), me // 2
    x, y = lax.rem(chip, side), chip // side

    def device(row, column, which):
        return (row * side + column) * 2 + which

    line = [(me, right), (me, left)]
    neighbours = [(device(y, x, 1 - core), z)]
    if side > 1:
        for move in (1, side - 1):
            neighbours.append((device(y, lax.rem(x + move, side), core), z))
            neighbours.append((device(lax.rem(y + move, side), x, core), z))

    def greet(sem, devices):
        for other in devices:
            pl.semaphore_signal(sem, inc=1, device_id=other, device_id_type=MESH)

    def meet(k):
        if k < near_rounds(NR):
            pl.semaphore_wait(near_sems.at[k], len(neighbours))
            if k + 1 < near_rounds(NR):
                greet(near_sems.at[k + 1], neighbours)

    def meet_line(k):
        if NZ >= 4 * (k + 1):
            pl.semaphore_wait(line_sems.at[k], 2)
        if k == 0 and NZ >= 8:
            for move in (2, NZ - 2):
                greet(line_sems.at[1], [(me, lax.rem(z + move, NZ))])

    barrier = pltpu.get_barrier_semaphore()
    greet(barrier, line + neighbours)
    pan_copies = [
        pltpu.make_async_copy(panel.at[pl.ds(h * HB, HB)], pan.at[z, h], pan_sem.at[h])
        for h in range(PARTS)
    ]
    for copy in pan_copies:
        copy.start()
    trl_copy = pltpu.make_async_copy(trailing, trl, trl_sem)
    trl_copy.start()
    pl.semaphore_wait(barrier, len(line + neighbours))

    def place(event, back, to_right):
        part = event % PARTS
        if to_right:
            return lax.rem(z - event // PARTS - back + NZ, NZ), part
        return lax.rem(z + event // PARTS + back, NZ), PARTS - 1 - part

    def send(event, own=False):
        for to_right in (True, False):
            origin, slot = place(event, 0, to_right)
            here = pan.at[origin, slot]
            pltpu.make_async_remote_copy(
                src_ref=panel.at[pl.ds(slot * HB, HB)] if own else here,
                dst_ref=here,
                send_sem=(right_send if to_right else left_send).at[event],
                recv_sem=(right_recv if to_right else left_recv).at[event],
                device_id=(me, right if to_right else left),
                device_id_type=MESH,
            ).start()

    def sent(ref, sem):
        pltpu.make_async_copy(ref, ref, sem).wait()

    if NZ >= 4:
        greet(line_sems.at[0], line)
    for event in range(PARTS // 2):
        send(event, own=True)
    if near_rounds(NR):
        greet(near_sems.at[0], neighbours)

    def rows_of(origin, slot):
        return pl.ds(pl.multiple_of((origin * PARTS + slot) * HB, HB), HB)

    def multiply(origin, slot):
        split = split_terms(pan[origin, slot])
        terms[rows_of(origin, slot), :] = split
        product = contract_rows(split, split_terms(trl[rows_of(origin, slot), :]))
        cacc[...] += (
            product[:WIDTH, :WIDTH] + product[WIDTH:, :WIDTH] + product[:WIDTH, WIDTH:]
        )

    def handle(event, forward):
        for from_left in (True, False):
            origin, slot = place(event, 1, from_left)
            sent(pan.at[origin, slot], (right_recv if from_left else left_recv).at[event])
        if forward:

            @pl.when(event + PARTS < events)
            def _():
                send(event + PARTS)

        for from_left in (True, False):
            multiply(*place(event, 1, from_left))

    def handle_range(first, last, forward=True):
        def one(event, carry):
            handle(event, forward)
            return carry

        if first < min(last, events):
            lax.fori_loop(first, min(last, events), one, 0)

    def forward_range(first, last):
        for event in range(first, min(last, events)):
            send(event)

    def scatter_start(source, landing, sems):
        def one(index, carry):
            owner = index * step
            part = source.at[pl.ds(pl.multiple_of(index * tile, tile), tile)]

            @pl.when(owner == me)
            def _():
                pltpu.make_async_copy(part, landing.at[me], sems.at[1]).start()

            @pl.when(owner != me)
            def _():
                pltpu.make_async_remote_copy(
                    src_ref=part,
                    dst_ref=landing.at[me],
                    send_sem=sems.at[0],
                    recv_sem=sems.at[1],
                    device_id=(owner, z),
                    device_id_type=MESH,
                ).start()

            return carry

        lax.fori_loop(0, owners, one, 0)

    def total(landing, count):
        value = landing[0]
        for k in range(1, count):
            value = value + landing[k]
        return value

    def scatter_finish(source, landing, sems):
        pltpu.make_async_copy(landing, landing, sems.at[1]).wait()
        return total(landing, NR)

    def spread_start(source, whole, sems):
        part = whole.at[pl.ds(pl.multiple_of(mine * tile, tile), tile)]
        pltpu.make_async_copy(source, part, sems.at[3]).start()

        def one(k, carry):
            pltpu.make_async_remote_copy(
                src_ref=source,
                dst_ref=part,
                send_sem=sems.at[2],
                recv_sem=sems.at[3],
                device_id=(lax.rem(me + k, NR), z),
                device_id_type=MESH,
            ).start()
            return carry

        lax.fori_loop(1, NR, one, 0)

    for copy in pan_copies:
        copy.wait()
    gram = None
    for h in range(PARTS):
        own = pan[z, h]
        part = contract_rows(own, own, HIGHEST)
        gram = part if gram is None else gram + part
    gram_local[...] = gram
    cacc[...] = jnp.zeros_like(cacc)
    meet(0)
    meet_line(0)
    for event in range(PARTS // 2, min(PARTS, events)):
        send(event, own=True)
    trl_copy.wait()
    for h in range(PARTS):
        multiply(z, h)
    meet(1)
    meet(2)
    handle_range(0, 1, forward=False)
    meet(3)
    scatter_start(gram_local, gram_terms, gram_sems)
    handle_range(1, 2, forward=False)
    forward_range(PARTS, PARTS + 1)
    handle_range(2, 3, forward=False)
    meet_line(1)

    @pl.when(is_owner)
    def _():
        gram_zsum[...] = scatter_finish(gram_local, gram_terms, gram_sems)
        pltpu.make_async_copy(gram_zsum, gram_z.at[z], gram_sems.at[5]).start()

        def one(k, carry):
            pltpu.make_async_remote_copy(
                src_ref=gram_zsum,
                dst_ref=gram_z.at[z],
                send_sem=gram_sems.at[4],
                recv_sem=gram_sems.at[5],
                device_id=(me, lax.rem(z + k, NZ)),
                device_id_type=MESH,
            ).start()
            return carry

        lax.fori_loop(1, NZ, one, 0)

    forward_range(PARTS + 1, PARTS + 3)
    handle_range(3, 6)

    @pl.when(is_owner)
    def _():
        pltpu.make_async_copy(gram_z, gram_z, gram_sems.at[5]).wait()
        gram_sum[...] = total(gram_z, NZ)
        spread_start(gram_sum, gram_whole, gram_sems)

    handle_range(6, 8)
    pltpu.make_async_copy(gram_whole, gram_whole, gram_sems.at[3]).wait()
    row_index = lax.broadcasted_iota(jnp.int32, (WIDTH, WIDTH), 0)
    column_index = lax.broadcasted_iota(jnp.int32, (WIDTH, WIDTH), 1)
    work[:, :WIDTH] = gram_whole[...]
    work[:, WIDTH:] = jnp.where(row_index == column_index, 1.0, 0.0).astype(jnp.float32)
    blocks = WIDTH // BLOCK

    def eliminate_part(part, carry):
        eliminate(work, part * (blocks // 4), blocks // 4)

        @pl.when(part + 8 < events)
        def _():
            handle(part + 8, True)

        return carry

    lax.fori_loop(0, 4, eliminate_part, 0)
    upper = jnp.where(row_index <= column_index, work[:, :WIDTH], 0.0)
    diagonal = jnp.sum(
        jnp.where(row_index == column_index, upper, 0.0), axis=1, keepdims=True
    )
    factor_out[...] = upper / jnp.sqrt(diagonal)
    work[:, WIDTH:] = work[:, WIDTH:] / jnp.sqrt(diagonal)
    twice(pair, work[:, WIDTH:].T)

    def to_basis(first, last):
        size = HB * PARTS // 2

        def one(index, carry):
            rows = pl.ds(pl.multiple_of(index * size, size), size)
            product = jnp.dot(terms[rows, :], pair[...], preferred_element_type=jnp.float32)
            terms[rows, :] = split_terms(product[:, :WIDTH] + product[:, WIDTH:])
            return carry

        lax.fori_loop(first, last, one, 0)

    handle_range(12, events, forward=False)

    moves = sorted(range(1, side), key=lambda move: -min(move, side - move))
    deep = WIDTH // 2
    first, second = prod_sems.at[0], prod_sems.at[1]
    along, across = jnp.where(core == 0, x, y), jnp.where(core == 0, y, x)
    sibling = device(y, x, 1 - core)

    def half(which):
        return pl.ds(pl.multiple_of(which * deep, deep), deep)

    def deliver(source, target, sems, peer):
        pltpu.make_async_remote_copy(
            src_ref=source,
            dst_ref=target,
            send_sem=sems.at[0],
            recv_sem=sems.at[1],
            device_id=(peer, z),
            device_id_type=MESH,
        ).start()

    for move in moves:
        along_x, along_y = lax.rem(x + move, side), lax.rem(y + move, side)
        deliver(cacc.at[:deep], line_terms.at[x * 2 + core], first, device(y, along_x, 0))
        deliver(cacc.at[deep:], line_terms.at[y * 2 + core], first, device(along_y, x, 1))
    deliver(cacc.at[half(1 - core)], line_terms.at[across * 2 + core], first, sibling)
    line_terms[along * 2 + core] = cacc[half(core), :]

    def ring_sent(event, carry):
        sent(pan.at[0, 0], right_send.at[event])
        sent(pan.at[0, 0], left_send.at[event])
        return carry

    lax.fori_loop(0, events, ring_sent, 0)

    @pl.when(is_owner)
    def _():
        sent(gram_local.at[: WIDTH - tile], gram_sems.at[0])
        sent(gram_terms.at[: NR - 1], gram_sems.at[2])
        sent(gram_z.at[: NZ - 1], gram_sems.at[4])

    @pl.when(jnp.logical_not(is_owner))
    def _():
        sent(gram_local, gram_sems.at[0])

    others = line_terms.at[: 2 * side - 1]
    to_basis(0, NZ)
    sent(others, first.at[1])
    half_sum[...] = total(line_terms, 2 * side)
    for move in moves:
        far_y = jnp.where(core == 0, lax.rem(y + move, side), y)
        far_x = jnp.where(core == 0, x, lax.rem(x + move, side))
        for which in range(2):
            deliver(half_sum, cross_terms.at[core, across], second, device(far_y, far_x, which))
    deliver(half_sum, cross_terms.at[core, across], second, sibling)
    cross_terms[core, across] = half_sum[...]
    sent(others, first.at[0])
    to_basis(NZ, 2 * NZ)
    sent(others, second.at[1])
    prod_whole[:deep, :] = total(cross_terms.at[0], side)
    prod_whole[deep:, :] = total(cross_terms.at[1], side)
    inverse_t = work[:, WIDTH:]
    coupling_out[...] = jnp.dot(
        inverse_t, prod_whole[...], precision=HIGHEST, preferred_element_type=jnp.float32
    )

    sent(others, second.at[0])


def apply_kernel(size, terms, trailing, factor, coupling, updated, factor_out, coupling_out, pair, held, sem, small_sem):
    factor_copy = pltpu.make_async_copy(factor, factor_out, small_sem.at[0])
    coupling_copy = pltpu.make_async_copy(coupling, coupling_out, small_sem.at[1])
    factor_copy.start()
    coupling_copy.start()
    twice(pair, coupling[...])
    for start in range(0, held.shape[0], size):
        rows = pl.ds(start, size)
        product = jnp.dot(terms[rows, :], pair[...], preferred_element_type=jnp.float32)
        held[rows, :] = trailing[rows, :] - (product[:, :WIDTH] + product[:, WIDTH:])
        pltpu.make_async_copy(held.at[rows], updated.at[rows], sem).start()
    pltpu.make_async_copy(held, updated, sem).wait()
    factor_copy.wait()
    coupling_copy.wait()


def per_device(NR, NZ, panel, trailing):
    HB = panel.shape[0] // PARTS
    rows = trailing.shape[0]
    owners = min(NR, 16)
    tile = WIDTH // owners
    events = ring_events(NZ)
    side = plane_side(NR)
    f32 = jnp.float32
    square = pltpu.VMEM((WIDTH, WIDTH), f32)
    small = jax.ShapeDtypeStruct((WIDTH, WIDTH), f32)
    kept_terms = pltpu.VMEM((rows, 2 * WIDTH), jnp.bfloat16)
    kept_rows = pltpu.VMEM((rows, WIDTH), f32)
    in_vmem = pl.BlockSpec(memory_space=pltpu.VMEM)
    anywhere = pl.BlockSpec(memory_space=pl.ANY)
    dma = pltpu.SemaphoreType.DMA
    factor, coupling, terms, kept = pl.pallas_call(
        functools.partial(main_kernel, NR, NZ, HB),
        out_shape=(square, square, kept_terms, kept_rows),
        in_specs=[anywhere, anywhere],
        out_specs=(in_vmem,) * 4,
        scratch_shapes=[
            pltpu.VMEM((NZ, PARTS, HB, WIDTH), f32),
            square,
            square,
            pltpu.VMEM((NR, tile, WIDTH), f32),
            pltpu.VMEM((NZ, tile, WIDTH), f32),
            pltpu.VMEM((tile, WIDTH), f32),
            pltpu.VMEM((tile, WIDTH), f32),
            square,
            pltpu.VMEM((2 * side, WIDTH // 2, WIDTH), f32),
            pltpu.VMEM((WIDTH // 2, WIDTH), f32),
            pltpu.VMEM((2, side, WIDTH // 2, WIDTH), f32),
            square,
            pltpu.VMEM((WIDTH, 2 * WIDTH), f32),
            pltpu.VMEM((2 * WIDTH, 2 * WIDTH), jnp.bfloat16),
            dma((PARTS,)),
            dma,
            dma((events,)),
            dma((events,)),
            dma((events,)),
            dma((events,)),
            dma((6,)),
            dma((2, 2)),
            pltpu.SemaphoreType.REGULAR((max(near_rounds(NR), 1),)),
            pltpu.SemaphoreType.REGULAR((2,)),
        ],
        compiler_params=pltpu.CompilerParams(
            collective_id=0, has_side_effects=True, vmem_limit_bytes=MAIN_VMEM
        ),
        name="gather_factor_couple",
    )(panel, trailing)
    updated, factor, coupling = pl.pallas_call(
        functools.partial(apply_kernel, min(rows, 128)),
        out_shape=(jax.ShapeDtypeStruct(trailing.shape, f32), small, small),
        in_specs=[in_vmem] * 4,
        out_specs=(anywhere,) * 3,
        scratch_shapes=[
            pltpu.VMEM((2 * WIDTH, 2 * WIDTH), jnp.bfloat16),
            pltpu.VMEM((rows, WIDTH), f32),
            dma,
            dma((2,)),
        ],
        compiler_params=pltpu.CompilerParams(vmem_limit_bytes=APPLY_VMEM),
        name="apply_update",
    )(terms, kept, factor, coupling)
    return factor, coupling, updated


def solution(mesh):
    return jax.shard_map(
        functools.partial(per_device, mesh.shape["rows"], mesh.shape["cols"]),
        mesh=mesh,
        in_specs=(P(("rows", "cols"), None), P("rows", "cols")),
        out_specs=(P(), P(None, "cols"), P("rows", "cols")),
        check_vma=False,
    )
```

```python
import functools

import jax
import jax.numpy as jnp
from jax import lax
from jax.experimental import pallas as pl
from jax.experimental.pallas import tpu as pltpu
from jax.sharding import PartitionSpec as P

MESH = pl.DeviceIdType.MESH
HIGHEST = lax.Precision.HIGHEST
WIDTH = 128
BLOCK = 8
PARTS = 4
MAIN_VMEM = 52 * 1024 * 1024
APPLY_VMEM = 16 * 1024 * 1024


def split_terms(value):
    high = value.astype(jnp.bfloat16)
    low = (value - high.astype(jnp.float32)).astype(jnp.bfloat16)
    return jnp.concatenate([high, low], axis=1)


def twice(pair, value):
    split = split_terms(value)
    pair[:WIDTH, :] = split
    pair[WIDTH:, :] = split


def contract_rows(left, right, precision=None):
    return lax.dot_general(
        left,
        right,
        (((0,), (0,)), ((), ())),
        precision=precision,
        preferred_element_type=jnp.float32,
    )


def eliminate(work, first, count):
    lane = lax.broadcasted_iota(jnp.int32, (BLOCK, WIDTH), 1)
    sub = lax.broadcasted_iota(jnp.int32, (BLOCK, WIDTH), 0)

    def one_block(index, carry):
        start = pl.multiple_of((first + index) * BLOCK, BLOCK)
        rows = work[pl.ds(start, BLOCK), :]
        gram_part = rows[:, :WIDTH]
        columns = []
        for a in range(BLOCK):
            picked = jnp.where(lane == start + a, gram_part, 0.0)
            column = jnp.sum(picked, axis=1, keepdims=True)
            columns.append(jnp.broadcast_to(column, (BLOCK, WIDTH)))
        scale = jnp.zeros((BLOCK, WIDTH), jnp.float32)
        for a in range(BLOCK):
            inverse = 1.0 / jnp.broadcast_to(columns[a][a : a + 1, :], (BLOCK, WIDTH))
            scale = jnp.where(sub == a, inverse, scale)
            factor = jnp.where(sub > a, columns[a] * inverse, 0.0)
            for d in range(a + 1, BLOCK):
                pivot_row = jnp.broadcast_to(columns[d][a : a + 1, :], (BLOCK, WIDTH))
                columns[d] = columns[d] - factor * pivot_row
            pivot_row = jnp.broadcast_to(rows[a : a + 1, :], (BLOCK, 2 * WIDTH))
            rows = rows - jnp.concatenate([factor, factor], axis=1) * pivot_row
        work[pl.ds(start, BLOCK), :] = rows
        lower = jnp.where(lane >= start + BLOCK, rows[:, :WIDTH] * scale, 0.0)
        work[...] = work[...] - contract_rows(lower, rows, HIGHEST)
        return carry

    lax.fori_loop(0, count, one_block, 0)


def plane_side(NR):
    side = 1
    while side * side * 2 < NR:
        side *= 2
    return side


def ring_events(NZ):
    return PARTS * (NZ // 2 - 1) + PARTS // 2


def near_rounds(NR):
    return 2 * (plane_side(NR) // 2)


def main_kernel(
    NR, NZ, HB,
    panel, trailing,
    factor_out, coupling_out, terms, trl,
    pan, cacc,
    gram_local, gram_terms, gram_z, gram_zsum, gram_sum, gram_whole,
    line_terms, half_sum, cross_terms, prod_whole, work, pair,
    pan_sem, trl_sem,
    right_send, right_recv, left_send, left_recv,
    gram_sems, prod_sems, near_sems, line_sems,
):
    me = lax.axis_index("rows")
    z = lax.axis_index("cols")
    owners = min(NR, 16)
    step = NR // owners
    tile = WIDTH // owners
    is_owner = lax.rem(me, step) == 0
    mine = me // step
    events = ring_events(NZ)
    right, left = lax.rem(z + 1, NZ), lax.rem(z + NZ - 1, NZ)

    side, core, chip = plane_side(NR), lax.rem(me, 2), me // 2
    x, y = lax.rem(chip, side), chip // side

    def device(row, column, which):
        return (row * side + column) * 2 + which

    line = [(me, right), (me, left)]
    neighbours = [(device(y, x, 1 - core), z)]
    if side > 1:
        for move in (1, side - 1):
            neighbours.append((device(y, lax.rem(x + move, side), core), z))
            neighbours.append((device(lax.rem(y + move, side), x, core), z))

    def greet(sem, devices):
        for other in devices:
            pl.semaphore_signal(sem, inc=1, device_id=other, device_id_type=MESH)

    def meet(k):
        if k < near_rounds(NR):
            pl.semaphore_wait(near_sems.at[k], len(neighbours))
            if k + 1 < near_rounds(NR):
                greet(near_sems.at[k + 1], neighbours)

    def meet_line(k):
        if NZ >= 4 * (k + 1):
            pl.semaphore_wait(line_sems.at[k], 2)
        if k == 0 and NZ >= 8:
            for move in (2, NZ - 2):
                greet(line_sems.at[1], [(me, lax.rem(z + move, NZ))])

    barrier = pltpu.get_barrier_semaphore()
    greet(barrier, line + neighbours)
    pan_copies = [
        pltpu.make_async_copy(panel.at[pl.ds(h * HB, HB)], pan.at[z, h], pan_sem.at[h])
        for h in range(PARTS)
    ]
    for copy in pan_copies:
        copy.start()
    trl_copy = pltpu.make_async_copy(trailing, trl, trl_sem)
    trl_copy.start()
    pl.semaphore_wait(barrier, len(line + neighbours))

    def place(event, back, to_right):
        part = event % PARTS
        if to_right:
            return lax.rem(z - event // PARTS - back + NZ, NZ), part
        return lax.rem(z + event // PARTS + back, NZ), PARTS - 1 - part

    def send(event, own=False):
        for to_right in (True, False):
            origin, slot = place(event, 0, to_right)
            here = pan.at[origin, slot]
            pltpu.make_async_remote_copy(
                src_ref=panel.at[pl.ds(slot * HB, HB)] if own else here,
                dst_ref=here,
                send_sem=(right_send if to_right else left_send).at[event],
                recv_sem=(right_recv if to_right else left_recv).at[event],
                device_id=(me, right if to_right else left),
                device_id_type=MESH,
            ).start()

    def sent(ref, sem):
        pltpu.make_async_copy(ref, ref, sem).wait()

    last, cut = events - 1, HB // 2

    def send_piece(event, to_right, first, count):
        origin, slot = place(event, 0, to_right)
        piece = pan.at[origin, slot, pl.ds(first, count)]
        pltpu.make_async_remote_copy(
            src_ref=piece,
            dst_ref=piece,
            send_sem=(right_send if to_right else left_send).at[event],
            recv_sem=(right_recv if to_right else left_recv).at[event],
            device_id=(me, right if to_right else left),
            device_id_type=MESH,
        ).start()

    def send_last():
        @pl.when(right != 0)
        def _():
            send_piece(last, True, 0, HB)

        @pl.when(right == 0)
        def _():
            send_piece(last, True, 0, cut)

        send_piece(last, False, 0, HB)

    def send_extra():
        @pl.when(left == 0)
        def _():
            send_piece(events, False, cut, HB - cut)

    if NZ >= 4:
        greet(line_sems.at[0], line)
    for event in range(PARTS // 2):
        send(event, own=True)
    if near_rounds(NR):
        greet(near_sems.at[0], neighbours)

    def rows_of(origin, slot):
        return pl.ds(pl.multiple_of((origin * PARTS + slot) * HB, HB), HB)

    def multiply(origin, slot):
        split = split_terms(pan[origin, slot])
        terms[rows_of(origin, slot), :] = split
        product = contract_rows(split, split_terms(trl[rows_of(origin, slot), :]))
        cacc[...] += (
            product[:WIDTH, :WIDTH] + product[WIDTH:, :WIDTH] + product[:WIDTH, WIDTH:]
        )

    def handle(event, forward):
        origin, slot = place(event, 1, True)
        split = jnp.logical_and(event == last, z == 0)

        @pl.when(jnp.logical_not(split))
        def _():
            sent(pan.at[origin, slot], right_recv.at[event])

        @pl.when(split)
        def _():
            sent(pan.at[origin, slot, pl.ds(0, cut)], right_recv.at[event])
            sent(pan.at[origin, slot, pl.ds(cut, HB - cut)], left_recv.at[events])

        origin, slot = place(event, 1, False)
        sent(pan.at[origin, slot], left_recv.at[event])
        if forward:

            @pl.when(event + PARTS < last)
            def _():
                send(event + PARTS)

            @pl.when(event + PARTS == last)
            def _():
                send_last()

            @pl.when(event + PARTS == events)
            def _():
                send_extra()

        for from_left in (True, False):
            multiply(*place(event, 1, from_left))

    def handle_range(first, stop, forward=True):
        def one(event, carry):
            handle(event, forward)
            return carry

        if first < min(stop, events):
            lax.fori_loop(first, min(stop, events), one, 0)

    def forward_range(first, stop):
        for event in range(first, min(stop, events + 1)):
            if event < last:
                send(event)
            elif event == last:
                send_last()
            else:
                send_extra()

    def scatter_start(source, landing, sems):
        def one(index, carry):
            owner = index * step
            part = source.at[pl.ds(pl.multiple_of(index * tile, tile), tile)]

            @pl.when(owner == me)
            def _():
                pltpu.make_async_copy(part, landing.at[me], sems.at[1]).start()

            @pl.when(owner != me)
            def _():
                pltpu.make_async_remote_copy(
                    src_ref=part,
                    dst_ref=landing.at[me],
                    send_sem=sems.at[0],
                    recv_sem=sems.at[1],
                    device_id=(owner, z),
                    device_id_type=MESH,
                ).start()

            return carry

        lax.fori_loop(0, owners, one, 0)

    def total(landing, count):
        value = landing[0]
        for k in range(1, count):
            value = value + landing[k]
        return value

    def scatter_finish(source, landing, sems):
        pltpu.make_async_copy(landing, landing, sems.at[1]).wait()
        return total(landing, NR)

    def spread_start(source, whole, sems):
        part = whole.at[pl.ds(pl.multiple_of(mine * tile, tile), tile)]
        pltpu.make_async_copy(source, part, sems.at[3]).start()

        def one(k, carry):
            pltpu.make_async_remote_copy(
                src_ref=source,
                dst_ref=part,
                send_sem=sems.at[2],
                recv_sem=sems.at[3],
                device_id=(lax.rem(me + k, NR), z),
                device_id_type=MESH,
            ).start()
            return carry

        lax.fori_loop(1, NR, one, 0)

    for copy in pan_copies:
        copy.wait()
    gram = None
    for h in range(PARTS):
        own = pan[z, h]
        part = contract_rows(own, own, HIGHEST)
        gram = part if gram is None else gram + part
    gram_local[...] = gram
    cacc[...] = jnp.zeros_like(cacc)
    meet(0)
    meet_line(0)
    for event in range(PARTS // 2, min(PARTS, events)):
        send(event, own=True)
    trl_copy.wait()
    for h in range(PARTS):
        multiply(z, h)
    meet(1)
    meet(2)
    handle_range(0, 1, forward=False)
    meet(3)
    scatter_start(gram_local, gram_terms, gram_sems)
    handle_range(1, 2, forward=False)
    forward_range(PARTS, PARTS + 1)
    handle_range(2, 3, forward=False)
    meet_line(1)

    @pl.when(is_owner)
    def _():
        gram_zsum[...] = scatter_finish(gram_local, gram_terms, gram_sems)
        pltpu.make_async_copy(gram_zsum, gram_z.at[z], gram_sems.at[5]).start()

        def one(k, carry):
            pltpu.make_async_remote_copy(
                src_ref=gram_zsum,
                dst_ref=gram_z.at[z],
                send_sem=gram_sems.at[4],
                recv_sem=gram_sems.at[5],
                device_id=(me, lax.rem(z + k, NZ)),
                device_id_type=MESH,
            ).start()
            return carry

        lax.fori_loop(1, NZ, one, 0)

    forward_range(PARTS + 1, PARTS + 3)
    handle_range(3, 6)

    @pl.when(is_owner)
    def _():
        pltpu.make_async_copy(gram_z, gram_z, gram_sems.at[5]).wait()
        gram_sum[...] = total(gram_z, NZ)
        spread_start(gram_sum, gram_whole, gram_sems)

    handle_range(6, 8)
    pltpu.make_async_copy(gram_whole, gram_whole, gram_sems.at[3]).wait()
    row_index = lax.broadcasted_iota(jnp.int32, (WIDTH, WIDTH), 0)
    column_index = lax.broadcasted_iota(jnp.int32, (WIDTH, WIDTH), 1)
    work[:, :WIDTH] = gram_whole[...]
    work[:, WIDTH:] = jnp.where(row_index == column_index, 1.0, 0.0).astype(jnp.float32)
    blocks = WIDTH // BLOCK

    def eliminate_part(part, carry):
        eliminate(work, part * (blocks // 4), blocks // 4)

        @pl.when(part + 8 < events)
        def _():
            handle(part + 8, True)

        return carry

    lax.fori_loop(0, 4, eliminate_part, 0)
    upper = jnp.where(row_index <= column_index, work[:, :WIDTH], 0.0)
    diagonal = jnp.sum(
        jnp.where(row_index == column_index, upper, 0.0), axis=1, keepdims=True
    )
    factor_out[...] = upper / jnp.sqrt(diagonal)
    work[:, WIDTH:] = work[:, WIDTH:] / jnp.sqrt(diagonal)
    twice(pair, work[:, WIDTH:].T)

    def to_basis(first, last):
        size = HB * PARTS // 2

        def one(index, carry):
            rows = pl.ds(pl.multiple_of(index * size, size), size)
            product = jnp.dot(terms[rows, :], pair[...], preferred_element_type=jnp.float32)
            terms[rows, :] = split_terms(product[:, :WIDTH] + product[:, WIDTH:])
            return carry

        lax.fori_loop(first, last, one, 0)

    handle_range(12, events, forward=False)

    moves = sorted(range(1, side), key=lambda move: -min(move, side - move))
    deep = WIDTH // 2
    first, second = prod_sems.at[0], prod_sems.at[1]
    along, across = jnp.where(core == 0, x, y), jnp.where(core == 0, y, x)
    sibling = device(y, x, 1 - core)

    def half(which):
        return pl.ds(pl.multiple_of(which * deep, deep), deep)

    def deliver(source, target, sems, peer):
        pltpu.make_async_remote_copy(
            src_ref=source,
            dst_ref=target,
            send_sem=sems.at[0],
            recv_sem=sems.at[1],
            device_id=(peer, z),
            device_id_type=MESH,
        ).start()

    for move in moves:
        along_x, along_y = lax.rem(x + move, side), lax.rem(y + move, side)
        deliver(cacc.at[:deep], line_terms.at[x * 2 + core], first, device(y, along_x, 0))
        deliver(cacc.at[deep:], line_terms.at[y * 2 + core], first, device(along_y, x, 1))
    deliver(cacc.at[half(1 - core)], line_terms.at[across * 2 + core], first, sibling)
    line_terms[along * 2 + core] = cacc[half(core), :]

    def ring_sent(event, carry):
        sent(pan.at[0, 0], right_send.at[event])
        sent(pan.at[0, 0], left_send.at[event])
        return carry

    lax.fori_loop(0, last, ring_sent, 0)
    sent(pan.at[0, 0], left_send.at[last])

    @pl.when(right != 0)
    def _():
        sent(pan.at[0, 0], right_send.at[last])

    @pl.when(right == 0)
    def _():
        sent(pan.at[0, 0, pl.ds(0, cut)], right_send.at[last])

    @pl.when(left == 0)
    def _():
        sent(pan.at[0, 0, pl.ds(cut, HB - cut)], left_send.at[events])

    @pl.when(is_owner)
    def _():
        sent(gram_local.at[: WIDTH - tile], gram_sems.at[0])
        sent(gram_terms.at[: NR - 1], gram_sems.at[2])
        sent(gram_z.at[: NZ - 1], gram_sems.at[4])

    @pl.when(jnp.logical_not(is_owner))
    def _():
        sent(gram_local, gram_sems.at[0])

    others = line_terms.at[: 2 * side - 1]
    to_basis(0, NZ)
    sent(others, first.at[1])
    half_sum[...] = total(line_terms, 2 * side)
    for move in moves:
        far_y = jnp.where(core == 0, lax.rem(y + move, side), y)
        far_x = jnp.where(core == 0, x, lax.rem(x + move, side))
        for which in range(2):
            deliver(half_sum, cross_terms.at[core, across], second, device(far_y, far_x, which))
    deliver(half_sum, cross_terms.at[core, across], second, sibling)
    cross_terms[core, across] = half_sum[...]
    sent(others, first.at[0])
    to_basis(NZ, 2 * NZ)
    sent(others, second.at[1])
    prod_whole[:deep, :] = total(cross_terms.at[0], side)
    prod_whole[deep:, :] = total(cross_terms.at[1], side)
    inverse_t = work[:, WIDTH:]
    coupling_out[...] = jnp.dot(
        inverse_t, prod_whole[...], precision=HIGHEST, preferred_element_type=jnp.float32
    )

    sent(others, second.at[0])


def apply_kernel(size, terms, trailing, factor, coupling, updated, factor_out, coupling_out, pair, held, sem, small_sem):
    factor_copy = pltpu.make_async_copy(factor, factor_out, small_sem.at[0])
    coupling_copy = pltpu.make_async_copy(coupling, coupling_out, small_sem.at[1])
    factor_copy.start()
    coupling_copy.start()
    twice(pair, coupling[...])
    for start in range(0, held.shape[0], size):
        rows = pl.ds(start, size)
        product = jnp.dot(terms[rows, :], pair[...], preferred_element_type=jnp.float32)
        held[rows, :] = trailing[rows, :] - (product[:, :WIDTH] + product[:, WIDTH:])
        pltpu.make_async_copy(held.at[rows], updated.at[rows], sem).start()
    pltpu.make_async_copy(held, updated, sem).wait()
    factor_copy.wait()
    coupling_copy.wait()


def per_device(NR, NZ, panel, trailing):
    HB = panel.shape[0] // PARTS
    rows = trailing.shape[0]
    owners = min(NR, 16)
    tile = WIDTH // owners
    events = ring_events(NZ)
    side = plane_side(NR)
    f32 = jnp.float32
    square = pltpu.VMEM((WIDTH, WIDTH), f32)
    small = jax.ShapeDtypeStruct((WIDTH, WIDTH), f32)
    kept_terms = pltpu.VMEM((rows, 2 * WIDTH), jnp.bfloat16)
    kept_rows = pltpu.VMEM((rows, WIDTH), f32)
    in_vmem = pl.BlockSpec(memory_space=pltpu.VMEM)
    anywhere = pl.BlockSpec(memory_space=pl.ANY)
    dma = pltpu.SemaphoreType.DMA
    factor, coupling, terms, kept = pl.pallas_call(
        functools.partial(main_kernel, NR, NZ, HB),
        out_shape=(square, square, kept_terms, kept_rows),
        in_specs=[anywhere, anywhere],
        out_specs=(in_vmem,) * 4,
        scratch_shapes=[
            pltpu.VMEM((NZ, PARTS, HB, WIDTH), f32),
            square,
            square,
            pltpu.VMEM((NR, tile, WIDTH), f32),
            pltpu.VMEM((NZ, tile, WIDTH), f32),
            pltpu.VMEM((tile, WIDTH), f32),
            pltpu.VMEM((tile, WIDTH), f32),
            square,
            pltpu.VMEM((2 * side, WIDTH // 2, WIDTH), f32),
            pltpu.VMEM((WIDTH // 2, WIDTH), f32),
            pltpu.VMEM((2, side, WIDTH // 2, WIDTH), f32),
            square,
            pltpu.VMEM((WIDTH, 2 * WIDTH), f32),
            pltpu.VMEM((2 * WIDTH, 2 * WIDTH), jnp.bfloat16),
            dma((PARTS,)),
            dma,
            dma((events + 1,)),
            dma((events + 1,)),
            dma((events + 1,)),
            dma((events + 1,)),
            dma((6,)),
            dma((2, 2)),
            pltpu.SemaphoreType.REGULAR((max(near_rounds(NR), 1),)),
            pltpu.SemaphoreType.REGULAR((2,)),
        ],
        compiler_params=pltpu.CompilerParams(
            collective_id=0, has_side_effects=True, vmem_limit_bytes=MAIN_VMEM
        ),
        name="gather_factor_couple",
    )(panel, trailing)
    updated, factor, coupling = pl.pallas_call(
        functools.partial(apply_kernel, min(rows, 128)),
        out_shape=(jax.ShapeDtypeStruct(trailing.shape, f32), small, small),
        in_specs=[in_vmem] * 4,
        out_specs=(anywhere,) * 3,
        scratch_shapes=[
            pltpu.VMEM((2 * WIDTH, 2 * WIDTH), jnp.bfloat16),
            pltpu.VMEM((rows, WIDTH), f32),
            dma,
            dma((2,)),
        ],
        compiler_params=pltpu.CompilerParams(vmem_limit_bytes=APPLY_VMEM),
        name="apply_update",
    )(terms, kept, factor, coupling)
    return factor, coupling, updated


def solution(mesh):
    return jax.shard_map(
        functools.partial(per_device, mesh.shape["rows"], mesh.shape["cols"]),
        mesh=mesh,
        in_specs=(P(("rows", "cols"), None), P("rows", "cols")),
        out_specs=(P(), P(None, "cols"), P("rows", "cols")),
        check_vma=False,
    )
```

```python
import functools

import jax
import jax.numpy as jnp
from jax import lax
from jax.experimental import pallas as pl
from jax.experimental.pallas import tpu as pltpu
from jax.sharding import PartitionSpec as P

MESH = pl.DeviceIdType.MESH
HIGHEST = lax.Precision.HIGHEST
WIDTH = 128
BLOCK = 16
PARTS = 4
MAIN_VMEM = 52 * 1024 * 1024
APPLY_VMEM = 16 * 1024 * 1024


def split_terms(value):
    high = value.astype(jnp.bfloat16)
    low = (value - high.astype(jnp.float32)).astype(jnp.bfloat16)
    return jnp.concatenate([high, low], axis=1)


def twice(pair, value):
    split = split_terms(value)
    pair[:WIDTH, :] = split
    pair[WIDTH:, :] = split


def contract_rows(left, right, precision=None):
    return lax.dot_general(
        left,
        right,
        (((0,), (0,)), ((), ())),
        precision=precision,
        preferred_element_type=jnp.float32,
    )


def eliminate(work, first, count):
    lane = lax.broadcasted_iota(jnp.int32, (BLOCK, WIDTH), 1)
    sub = lax.broadcasted_iota(jnp.int32, (BLOCK, WIDTH), 0)

    def one_block(index, carry):
        start = pl.multiple_of((first + index) * BLOCK, BLOCK)
        rows = work[pl.ds(start, BLOCK), :]
        gram_part = rows[:, :WIDTH]
        columns = []
        for a in range(BLOCK):
            picked = jnp.where(lane == start + a, gram_part, 0.0)
            column = jnp.sum(picked, axis=1, keepdims=True)
            columns.append(jnp.broadcast_to(column, (BLOCK, WIDTH)))
        scale = jnp.zeros((BLOCK, WIDTH), jnp.float32)
        for a in range(BLOCK):
            inverse = 1.0 / jnp.broadcast_to(columns[a][a : a + 1, :], (BLOCK, WIDTH))
            scale = jnp.where(sub == a, inverse, scale)
            factor = jnp.where(sub > a, columns[a] * inverse, 0.0)
            for d in range(a + 1, BLOCK):
                pivot_row = jnp.broadcast_to(columns[d][a : a + 1, :], (BLOCK, WIDTH))
                columns[d] = columns[d] - factor * pivot_row
            pivot_row = jnp.broadcast_to(rows[a : a + 1, :], (BLOCK, 2 * WIDTH))
            rows = rows - jnp.concatenate([factor, factor], axis=1) * pivot_row
        work[pl.ds(start, BLOCK), :] = rows
        lower = jnp.where(lane >= start + BLOCK, rows[:, :WIDTH] * scale, 0.0)
        work[...] = work[...] - contract_rows(lower, rows, HIGHEST)
        return carry

    lax.fori_loop(0, count, one_block, 0)


def plane_side(NR):
    side = 1
    while side * side * 2 < NR:
        side *= 2
    return side


def ring_events(NZ):
    return PARTS * (NZ // 2 - 1) + PARTS // 2


def near_rounds(NR):
    return 2 * (plane_side(NR) // 2)


def main_kernel(
    NR, NZ, HB,
    panel, trailing,
    factor_out, coupling_out, terms, trl,
    pan, cacc,
    gram_local, gram_terms, gram_z, gram_zsum, gram_sum, gram_whole,
    line_terms, half_sum, cross_terms, prod_whole, work, pair,
    pan_sem, trl_sem,
    right_send, right_recv, left_send, left_recv,
    gram_sems, prod_sems, near_sems, line_sems,
):
    me = lax.axis_index("rows")
    z = lax.axis_index("cols")
    owners = min(NR, 16)
    step = NR // owners
    tile = WIDTH // owners
    is_owner = lax.rem(me, step) == 0
    mine = me // step
    events = ring_events(NZ)
    right, left = lax.rem(z + 1, NZ), lax.rem(z + NZ - 1, NZ)

    side, core, chip = plane_side(NR), lax.rem(me, 2), me // 2
    x, y = lax.rem(chip, side), chip // side

    def device(row, column, which):
        return (row * side + column) * 2 + which

    line = [(me, right), (me, left)]
    neighbours = [(device(y, x, 1 - core), z)]
    if side > 1:
        for move in (1, side - 1):
            neighbours.append((device(y, lax.rem(x + move, side), core), z))
            neighbours.append((device(lax.rem(y + move, side), x, core), z))

    def greet(sem, devices):
        for other in devices:
            pl.semaphore_signal(sem, inc=1, device_id=other, device_id_type=MESH)

    def meet(k):
        if k < near_rounds(NR):
            pl.semaphore_wait(near_sems.at[k], len(neighbours))
            if k + 1 < near_rounds(NR):
                greet(near_sems.at[k + 1], neighbours)

    def meet_line(k):
        if NZ >= 4 * (k + 1):
            pl.semaphore_wait(line_sems.at[k], 2)
        if k == 0 and NZ >= 8:
            for move in (2, NZ - 2):
                greet(line_sems.at[1], [(me, lax.rem(z + move, NZ))])

    barrier = pltpu.get_barrier_semaphore()
    greet(barrier, line + neighbours)
    pan_copies = [
        pltpu.make_async_copy(panel.at[pl.ds(h * HB, HB)], pan.at[z, h], pan_sem.at[h])
        for h in range(PARTS)
    ]
    for copy in pan_copies:
        copy.start()
    trl_copy = pltpu.make_async_copy(trailing, trl, trl_sem)
    trl_copy.start()
    pl.semaphore_wait(barrier, len(line + neighbours))

    def place(event, back, to_right):
        part = event % PARTS
        if to_right:
            return lax.rem(z - event // PARTS - back + NZ, NZ), part
        return lax.rem(z + event // PARTS + back, NZ), PARTS - 1 - part

    def send(event, own=False):
        for to_right in (True, False):
            origin, slot = place(event, 0, to_right)
            here = pan.at[origin, slot]
            pltpu.make_async_remote_copy(
                src_ref=panel.at[pl.ds(slot * HB, HB)] if own else here,
                dst_ref=here,
                send_sem=(right_send if to_right else left_send).at[event],
                recv_sem=(right_recv if to_right else left_recv).at[event],
                device_id=(me, right if to_right else left),
                device_id_type=MESH,
            ).start()

    def sent(ref, sem):
        pltpu.make_async_copy(ref, ref, sem).wait()

    last, cut = events - 1, HB // 2

    def send_piece(event, to_right, first, count):
        origin, slot = place(event, 0, to_right)
        piece = pan.at[origin, slot, pl.ds(first, count)]
        pltpu.make_async_remote_copy(
            src_ref=piece,
            dst_ref=piece,
            send_sem=(right_send if to_right else left_send).at[event],
            recv_sem=(right_recv if to_right else left_recv).at[event],
            device_id=(me, right if to_right else left),
            device_id_type=MESH,
        ).start()

    def send_last():
        @pl.when(right != 0)
        def _():
            send_piece(last, True, 0, HB)

        @pl.when(right == 0)
        def _():
            send_piece(last, True, 0, cut)

        send_piece(last, False, 0, HB)

    def send_extra():
        @pl.when(left == 0)
        def _():
            send_piece(events, False, cut, HB - cut)

    if NZ >= 4:
        greet(line_sems.at[0], line)
    for event in range(PARTS // 2):
        send(event, own=True)
    if near_rounds(NR):
        greet(near_sems.at[0], neighbours)

    def rows_of(origin, slot):
        return pl.ds(pl.multiple_of((origin * PARTS + slot) * HB, HB), HB)

    def multiply(origin, slot):
        split = split_terms(pan[origin, slot])
        terms[rows_of(origin, slot), :] = split
        product = contract_rows(split, split_terms(trl[rows_of(origin, slot), :]))
        cacc[...] += (
            product[:WIDTH, :WIDTH] + product[WIDTH:, :WIDTH] + product[:WIDTH, WIDTH:]
        )

    def handle(event, forward):
        origin, slot = place(event, 1, True)
        split = jnp.logical_and(event == last, z == 0)

        @pl.when(jnp.logical_not(split))
        def _():
            sent(pan.at[origin, slot], right_recv.at[event])

        @pl.when(split)
        def _():
            sent(pan.at[origin, slot, pl.ds(0, cut)], right_recv.at[event])
            sent(pan.at[origin, slot, pl.ds(cut, HB - cut)], left_recv.at[events])

        origin, slot = place(event, 1, False)
        sent(pan.at[origin, slot], left_recv.at[event])
        if forward:

            @pl.when(event + PARTS < last)
            def _():
                send(event + PARTS)

            @pl.when(event + PARTS == last)
            def _():
                send_last()

            @pl.when(event + PARTS == events)
            def _():
                send_extra()

        for from_left in (True, False):
            multiply(*place(event, 1, from_left))

    def handle_range(first, stop, forward=True):
        def one(event, carry):
            handle(event, forward)
            return carry

        if first < min(stop, events):
            lax.fori_loop(first, min(stop, events), one, 0)

    def forward_range(first, stop):
        for event in range(first, min(stop, events + 1)):
            if event < last:
                send(event)
            elif event == last:
                send_last()
            else:
                send_extra()

    def scatter_start(source, landing, sems):
        def one(index, carry):
            owner = index * step
            part = source.at[pl.ds(pl.multiple_of(index * tile, tile), tile)]

            @pl.when(owner == me)
            def _():
                pltpu.make_async_copy(part, landing.at[me], sems.at[1]).start()

            @pl.when(owner != me)
            def _():
                pltpu.make_async_remote_copy(
                    src_ref=part,
                    dst_ref=landing.at[me],
                    send_sem=sems.at[0],
                    recv_sem=sems.at[1],
                    device_id=(owner, z),
                    device_id_type=MESH,
                ).start()

            return carry

        lax.fori_loop(0, owners, one, 0)

    def total(landing, count):
        value = landing[0]
        for k in range(1, count):
            value = value + landing[k]
        return value

    def scatter_finish(source, landing, sems):
        pltpu.make_async_copy(landing, landing, sems.at[1]).wait()
        return total(landing, NR)

    def spread_start(source, whole, sems):
        part = whole.at[pl.ds(pl.multiple_of(mine * tile, tile), tile)]
        pltpu.make_async_copy(source, part, sems.at[3]).start()

        def one(k, carry):
            pltpu.make_async_remote_copy(
                src_ref=source,
                dst_ref=part,
                send_sem=sems.at[2],
                recv_sem=sems.at[3],
                device_id=(lax.rem(me + k, NR), z),
                device_id_type=MESH,
            ).start()
            return carry

        lax.fori_loop(1, NR, one, 0)

    for copy in pan_copies:
        copy.wait()
    gram = None
    for h in range(PARTS):
        own = pan[z, h]
        part = contract_rows(own, own, HIGHEST)
        gram = part if gram is None else gram + part
    gram_local[...] = gram
    cacc[...] = jnp.zeros_like(cacc)
    meet(0)
    meet_line(0)
    for event in range(PARTS // 2, min(PARTS, events)):
        send(event, own=True)
    trl_copy.wait()
    for h in range(PARTS):
        multiply(z, h)
    meet(1)
    meet(2)
    handle_range(0, 1, forward=False)
    meet(3)
    scatter_start(gram_local, gram_terms, gram_sems)
    handle_range(1, 2, forward=False)
    forward_range(PARTS, PARTS + 1)
    handle_range(2, 3, forward=False)
    meet_line(1)

    @pl.when(is_owner)
    def _():
        gram_zsum[...] = scatter_finish(gram_local, gram_terms, gram_sems)
        pltpu.make_async_copy(gram_zsum, gram_z.at[z], gram_sems.at[5]).start()

        def one(k, carry):
            pltpu.make_async_remote_copy(
                src_ref=gram_zsum,
                dst_ref=gram_z.at[z],
                send_sem=gram_sems.at[4],
                recv_sem=gram_sems.at[5],
                device_id=(me, lax.rem(z + k, NZ)),
                device_id_type=MESH,
            ).start()
            return carry

        lax.fori_loop(1, NZ, one, 0)

    forward_range(PARTS + 1, PARTS + 3)
    handle_range(3, 6)

    @pl.when(is_owner)
    def _():
        pltpu.make_async_copy(gram_z, gram_z, gram_sems.at[5]).wait()
        gram_sum[...] = total(gram_z, NZ)
        spread_start(gram_sum, gram_whole, gram_sems)

    handle_range(6, 8)
    pltpu.make_async_copy(gram_whole, gram_whole, gram_sems.at[3]).wait()
    row_index = lax.broadcasted_iota(jnp.int32, (WIDTH, WIDTH), 0)
    column_index = lax.broadcasted_iota(jnp.int32, (WIDTH, WIDTH), 1)
    work[:, :WIDTH] = gram_whole[...]
    work[:, WIDTH:] = jnp.where(row_index == column_index, 1.0, 0.0).astype(jnp.float32)
    blocks = WIDTH // BLOCK

    def eliminate_part(part, carry):
        eliminate(work, part * (blocks // 4), blocks // 4)

        @pl.when(part + 8 < events)
        def _():
            handle(part + 8, True)

        return carry

    lax.fori_loop(0, 4, eliminate_part, 0)
    upper = jnp.where(row_index <= column_index, work[:, :WIDTH], 0.0)
    diagonal = jnp.sum(
        jnp.where(row_index == column_index, upper, 0.0), axis=1, keepdims=True
    )
    factor_out[...] = upper / jnp.sqrt(diagonal)
    work[:, WIDTH:] = work[:, WIDTH:] / jnp.sqrt(diagonal)
    twice(pair, work[:, WIDTH:].T)

    def to_basis(first, last):
        size = HB * PARTS // 2

        def one(index, carry):
            rows = pl.ds(pl.multiple_of(index * size, size), size)
            product = jnp.dot(terms[rows, :], pair[...], preferred_element_type=jnp.float32)
            terms[rows, :] = split_terms(product[:, :WIDTH] + product[:, WIDTH:])
            return carry

        lax.fori_loop(first, last, one, 0)

    handle_range(12, events, forward=False)

    moves = sorted(range(1, side), key=lambda move: -min(move, side - move))
    deep = WIDTH // 2
    first, second = prod_sems.at[0], prod_sems.at[1]
    along, across = jnp.where(core == 0, x, y), jnp.where(core == 0, y, x)
    sibling = device(y, x, 1 - core)

    def half(which):
        return pl.ds(pl.multiple_of(which * deep, deep), deep)

    def deliver(source, target, sems, peer):
        pltpu.make_async_remote_copy(
            src_ref=source,
            dst_ref=target,
            send_sem=sems.at[0],
            recv_sem=sems.at[1],
            device_id=(peer, z),
            device_id_type=MESH,
        ).start()

    for move in moves:
        along_x, along_y = lax.rem(x + move, side), lax.rem(y + move, side)
        deliver(cacc.at[:deep], line_terms.at[x * 2 + core], first, device(y, along_x, 0))
        deliver(cacc.at[deep:], line_terms.at[y * 2 + core], first, device(along_y, x, 1))
    deliver(cacc.at[half(1 - core)], line_terms.at[across * 2 + core], first, sibling)
    line_terms[along * 2 + core] = cacc[half(core), :]

    def ring_sent(event, carry):
        sent(pan.at[0, 0], right_send.at[event])
        sent(pan.at[0, 0], left_send.at[event])
        return carry

    lax.fori_loop(0, last, ring_sent, 0)
    sent(pan.at[0, 0], left_send.at[last])

    @pl.when(right != 0)
    def _():
        sent(pan.at[0, 0], right_send.at[last])

    @pl.when(right == 0)
    def _():
        sent(pan.at[0, 0, pl.ds(0, cut)], right_send.at[last])

    @pl.when(left == 0)
    def _():
        sent(pan.at[0, 0, pl.ds(cut, HB - cut)], left_send.at[events])

    @pl.when(is_owner)
    def _():
        sent(gram_local.at[: WIDTH - tile], gram_sems.at[0])
        sent(gram_terms.at[: NR - 1], gram_sems.at[2])
        sent(gram_z.at[: NZ - 1], gram_sems.at[4])

    @pl.when(jnp.logical_not(is_owner))
    def _():
        sent(gram_local, gram_sems.at[0])

    others = line_terms.at[: 2 * side - 1]
    to_basis(0, NZ)
    sent(others, first.at[1])
    half_sum[...] = total(line_terms, 2 * side)
    for move in moves:
        far_y = jnp.where(core == 0, lax.rem(y + move, side), y)
        far_x = jnp.where(core == 0, x, lax.rem(x + move, side))
        for which in range(2):
            deliver(half_sum, cross_terms.at[core, across], second, device(far_y, far_x, which))
    deliver(half_sum, cross_terms.at[core, across], second, sibling)
    cross_terms[core, across] = half_sum[...]
    sent(others, first.at[0])
    to_basis(NZ, 2 * NZ)
    sent(others, second.at[1])
    prod_whole[:deep, :] = total(cross_terms.at[0], side)
    prod_whole[deep:, :] = total(cross_terms.at[1], side)
    inverse_t = work[:, WIDTH:]
    coupling_out[...] = jnp.dot(
        inverse_t, prod_whole[...], precision=HIGHEST, preferred_element_type=jnp.float32
    )

    sent(others, second.at[0])


def apply_kernel(size, terms, trailing, factor, coupling, updated, factor_out, coupling_out, pair, held, sem, small_sem):
    factor_copy = pltpu.make_async_copy(factor, factor_out, small_sem.at[0])
    coupling_copy = pltpu.make_async_copy(coupling, coupling_out, small_sem.at[1])
    factor_copy.start()
    coupling_copy.start()
    twice(pair, coupling[...])
    for start in range(0, held.shape[0], size):
        rows = pl.ds(start, size)
        product = jnp.dot(terms[rows, :], pair[...], preferred_element_type=jnp.float32)
        held[rows, :] = trailing[rows, :] - (product[:, :WIDTH] + product[:, WIDTH:])
        pltpu.make_async_copy(held.at[rows], updated.at[rows], sem).start()
    pltpu.make_async_copy(held, updated, sem).wait()
    factor_copy.wait()
    coupling_copy.wait()


def per_device(NR, NZ, panel, trailing):
    HB = panel.shape[0] // PARTS
    rows = trailing.shape[0]
    owners = min(NR, 16)
    tile = WIDTH // owners
    events = ring_events(NZ)
    side = plane_side(NR)
    f32 = jnp.float32
    square = pltpu.VMEM((WIDTH, WIDTH), f32)
    small = jax.ShapeDtypeStruct((WIDTH, WIDTH), f32)
    kept_terms = pltpu.VMEM((rows, 2 * WIDTH), jnp.bfloat16)
    kept_rows = pltpu.VMEM((rows, WIDTH), f32)
    in_vmem = pl.BlockSpec(memory_space=pltpu.VMEM)
    anywhere = pl.BlockSpec(memory_space=pl.ANY)
    dma = pltpu.SemaphoreType.DMA
    factor, coupling, terms, kept = pl.pallas_call(
        functools.partial(main_kernel, NR, NZ, HB),
        out_shape=(square, square, kept_terms, kept_rows),
        in_specs=[anywhere, anywhere],
        out_specs=(in_vmem,) * 4,
        scratch_shapes=[
            pltpu.VMEM((NZ, PARTS, HB, WIDTH), f32),
            square,
            square,
            pltpu.VMEM((NR, tile, WIDTH), f32),
            pltpu.VMEM((NZ, tile, WIDTH), f32),
            pltpu.VMEM((tile, WIDTH), f32),
            pltpu.VMEM((tile, WIDTH), f32),
            square,
            pltpu.VMEM((2 * side, WIDTH // 2, WIDTH), f32),
            pltpu.VMEM((WIDTH // 2, WIDTH), f32),
            pltpu.VMEM((2, side, WIDTH // 2, WIDTH), f32),
            square,
            pltpu.VMEM((WIDTH, 2 * WIDTH), f32),
            pltpu.VMEM((2 * WIDTH, 2 * WIDTH), jnp.bfloat16),
            dma((PARTS,)),
            dma,
            dma((events + 1,)),
            dma((events + 1,)),
            dma((events + 1,)),
            dma((events + 1,)),
            dma((6,)),
            dma((2, 2)),
            pltpu.SemaphoreType.REGULAR((max(near_rounds(NR), 1),)),
            pltpu.SemaphoreType.REGULAR((2,)),
        ],
        compiler_params=pltpu.CompilerParams(
            collective_id=0, has_side_effects=True, vmem_limit_bytes=MAIN_VMEM
        ),
        name="gather_factor_couple",
    )(panel, trailing)
    updated, factor, coupling = pl.pallas_call(
        functools.partial(apply_kernel, min(rows, 128)),
        out_shape=(jax.ShapeDtypeStruct(trailing.shape, f32), small, small),
        in_specs=[in_vmem] * 4,
        out_specs=(anywhere,) * 3,
        scratch_shapes=[
            pltpu.VMEM((2 * WIDTH, 2 * WIDTH), jnp.bfloat16),
            pltpu.VMEM((rows, WIDTH), f32),
            dma,
            dma((2,)),
        ],
        compiler_params=pltpu.CompilerParams(vmem_limit_bytes=APPLY_VMEM),
        name="apply_update",
    )(terms, kept, factor, coupling)
    return factor, coupling, updated


def solution(mesh):
    return jax.shard_map(
        functools.partial(per_device, mesh.shape["rows"], mesh.shape["cols"]),
        mesh=mesh,
        in_specs=(P(("rows", "cols"), None), P("rows", "cols")),
        out_specs=(P(), P(None, "cols"), P("rows", "cols")),
        check_vma=False,
    )
```

```python
import functools

import jax
import jax.numpy as jnp
from jax import lax
from jax.experimental import pallas as pl
from jax.experimental.pallas import tpu as pltpu
from jax.sharding import PartitionSpec as P

MESH = pl.DeviceIdType.MESH
HIGHEST = lax.Precision.HIGHEST
WIDTH = 128
BLOCK = 8
PARTS = 4
MAIN_VMEM = 52 * 1024 * 1024
APPLY_VMEM = 16 * 1024 * 1024


def split_terms(value):
    high = value.astype(jnp.bfloat16)
    low = (value - high.astype(jnp.float32)).astype(jnp.bfloat16)
    return jnp.concatenate([high, low], axis=1)


def twice(pair, value):
    split = split_terms(value)
    pair[:WIDTH, :] = split
    pair[WIDTH:, :] = split


def contract_rows(left, right, precision=None):
    return lax.dot_general(
        left,
        right,
        (((0,), (0,)), ((), ())),
        precision=precision,
        preferred_element_type=jnp.float32,
    )


def eliminate(work, first, count):
    lane = lax.broadcasted_iota(jnp.int32, (BLOCK, WIDTH), 1)
    sub = lax.broadcasted_iota(jnp.int32, (BLOCK, WIDTH), 0)

    def one_block(index, carry):
        start = pl.multiple_of((first + index) * BLOCK, BLOCK)
        rows = work[pl.ds(start, BLOCK), :]
        gram_part = rows[:, :WIDTH]
        columns = []
        for a in range(BLOCK):
            picked = jnp.where(lane == start + a, gram_part, 0.0)
            column = jnp.sum(picked, axis=1, keepdims=True)
            columns.append(jnp.broadcast_to(column, (BLOCK, WIDTH)))
        scale = jnp.zeros((BLOCK, WIDTH), jnp.float32)
        for a in range(BLOCK):
            inverse = 1.0 / jnp.broadcast_to(columns[a][a : a + 1, :], (BLOCK, WIDTH))
            scale = jnp.where(sub == a, inverse, scale)
            factor = jnp.where(sub > a, columns[a] * inverse, 0.0)
            for d in range(a + 1, BLOCK):
                pivot_row = jnp.broadcast_to(columns[d][a : a + 1, :], (BLOCK, WIDTH))
                columns[d] = columns[d] - factor * pivot_row
            pivot_row = jnp.broadcast_to(rows[a : a + 1, :], (BLOCK, 2 * WIDTH))
            rows = rows - jnp.concatenate([factor, factor], axis=1) * pivot_row
        work[pl.ds(start, BLOCK), :] = rows
        lower = jnp.where(lane >= start + BLOCK, rows[:, :WIDTH] * scale, 0.0)
        work[...] = work[...] - contract_rows(lower, rows, HIGHEST)
        return carry

    lax.fori_loop(0, count, one_block, 0)


def plane_side(NR):
    side = 1
    while side * side * 2 < NR:
        side *= 2
    return side


def ring_events(NZ):
    return PARTS * (NZ // 2 - 1) + PARTS // 2


def near_rounds(NR):
    return 2 * (plane_side(NR) // 2)


def main_kernel(
    NR, NZ, HB,
    panel, trailing,
    factor_out, coupling_out, terms, trl,
    pan, cacc,
    gram_local, gram_terms, gram_z, gram_zsum, gram_sum, gram_whole,
    line_terms, half_sum, cross_terms, prod_whole, work, pair,
    pan_sem, trl_sem,
    right_send, right_recv, left_send, left_recv,
    gram_sems, prod_sems, near_sems, line_sems,
):
    me = lax.axis_index("rows")
    z = lax.axis_index("cols")
    owners = min(NR, 16)
    step = NR // owners
    tile = WIDTH // owners
    is_owner = lax.rem(me, step) == 0
    mine = me // step
    events = ring_events(NZ)
    right, left = lax.rem(z + 1, NZ), lax.rem(z + NZ - 1, NZ)

    side, core, chip = plane_side(NR), lax.rem(me, 2), me // 2
    x, y = lax.rem(chip, side), chip // side

    def device(row, column, which):
        return (row * side + column) * 2 + which

    line = [(me, right), (me, left)]
    neighbours = [(device(y, x, 1 - core), z)]
    if side > 1:
        for move in (1, side - 1):
            neighbours.append((device(y, lax.rem(x + move, side), core), z))
            neighbours.append((device(lax.rem(y + move, side), x, core), z))

    def greet(sem, devices):
        for other in devices:
            pl.semaphore_signal(sem, inc=1, device_id=other, device_id_type=MESH)

    def meet(k):
        if k < near_rounds(NR):
            pl.semaphore_wait(near_sems.at[k], len(neighbours))
            if k + 1 < near_rounds(NR):
                greet(near_sems.at[k + 1], neighbours)

    def meet_line(k):
        if NZ >= 4 * (k + 1):
            pl.semaphore_wait(line_sems.at[k], 2)
        if k == 0 and NZ >= 8:
            for move in (2, NZ - 2):
                greet(line_sems.at[1], [(me, lax.rem(z + move, NZ))])

    barrier = pltpu.get_barrier_semaphore()
    greet(barrier, line + neighbours)
    pl.semaphore_wait(barrier, len(line + neighbours))

    def place(event, back, to_right):
        part = event % PARTS
        if to_right:
            return lax.rem(z - event // PARTS - back + NZ, NZ), part
        return lax.rem(z + event // PARTS + back, NZ), PARTS - 1 - part

    def send(event, own=False):
        for to_right in (True, False):
            origin, slot = place(event, 0, to_right)
            here = pan.at[origin, slot]
            pltpu.make_async_remote_copy(
                src_ref=panel.at[pl.ds(slot * HB, HB)] if own else here,
                dst_ref=here,
                send_sem=(right_send if to_right else left_send).at[event],
                recv_sem=(right_recv if to_right else left_recv).at[event],
                device_id=(me, right if to_right else left),
                device_id_type=MESH,
            ).start()

    def sent(ref, sem):
        pltpu.make_async_copy(ref, ref, sem).wait()

    last, cut = events - 1, HB // 2

    def send_piece(event, to_right, first, count):
        origin, slot = place(event, 0, to_right)
        piece = pan.at[origin, slot, pl.ds(first, count)]
        pltpu.make_async_remote_copy(
            src_ref=piece,
            dst_ref=piece,
            send_sem=(right_send if to_right else left_send).at[event],
            recv_sem=(right_recv if to_right else left_recv).at[event],
            device_id=(me, right if to_right else left),
            device_id_type=MESH,
        ).start()

    def send_last():
        @pl.when(right != 0)
        def _():
            send_piece(last, True, 0, HB)

        @pl.when(right == 0)
        def _():
            send_piece(last, True, 0, cut)

        send_piece(last, False, 0, HB)

    def send_extra():
        @pl.when(left == 0)
        def _():
            send_piece(events, False, cut, HB - cut)

    if NZ >= 4:
        greet(line_sems.at[0], line)
    for event in range(PARTS // 2):
        send(event, own=True)
    pan_copies = [
        pltpu.make_async_copy(panel.at[pl.ds(h * HB, HB)], pan.at[z, h], pan_sem.at[h])
        for h in range(PARTS)
    ]
    for copy in pan_copies:
        copy.start()
    trl_copy = pltpu.make_async_copy(trailing, trl, trl_sem)
    trl_copy.start()
    if near_rounds(NR):
        greet(near_sems.at[0], neighbours)

    def rows_of(origin, slot):
        return pl.ds(pl.multiple_of((origin * PARTS + slot) * HB, HB), HB)

    def multiply(origin, slot):
        split = split_terms(pan[origin, slot])
        terms[rows_of(origin, slot), :] = split
        product = contract_rows(split, split_terms(trl[rows_of(origin, slot), :]))
        cacc[...] += (
            product[:WIDTH, :WIDTH] + product[WIDTH:, :WIDTH] + product[:WIDTH, WIDTH:]
        )

    def handle(event, forward):
        origin, slot = place(event, 1, True)
        split = jnp.logical_and(event == last, z == 0)

        @pl.when(jnp.logical_not(split))
        def _():
            sent(pan.at[origin, slot], right_recv.at[event])

        @pl.when(split)
        def _():
            sent(pan.at[origin, slot, pl.ds(0, cut)], right_recv.at[event])
            sent(pan.at[origin, slot, pl.ds(cut, HB - cut)], left_recv.at[events])

        origin, slot = place(event, 1, False)
        sent(pan.at[origin, slot], left_recv.at[event])
        if forward:

            @pl.when(event + PARTS < last)
            def _():
                send(event + PARTS)

            @pl.when(event + PARTS == last)
            def _():
                send_last()

            @pl.when(event + PARTS == events)
            def _():
                send_extra()

        for from_left in (True, False):
            multiply(*place(event, 1, from_left))

    def handle_range(first, stop, forward=True):
        def one(event, carry):
            handle(event, forward)
            return carry

        if first < min(stop, events):
            lax.fori_loop(first, min(stop, events), one, 0)

    def forward_range(first, stop):
        for event in range(first, min(stop, events + 1)):
            if event < last:
                send(event)
            elif event == last:
                send_last()
            else:
                send_extra()

    def scatter_start(source, landing, sems):
        def one(index, carry):
            owner = index * step
            part = source.at[pl.ds(pl.multiple_of(index * tile, tile), tile)]

            @pl.when(owner == me)
            def _():
                pltpu.make_async_copy(part, landing.at[me], sems.at[1]).start()

            @pl.when(owner != me)
            def _():
                pltpu.make_async_remote_copy(
                    src_ref=part,
                    dst_ref=landing.at[me],
                    send_sem=sems.at[0],
                    recv_sem=sems.at[1],
                    device_id=(owner, z),
                    device_id_type=MESH,
                ).start()

            return carry

        lax.fori_loop(0, owners, one, 0)

    def total(landing, count):
        value = landing[0]
        for k in range(1, count):
            value = value + landing[k]
        return value

    def scatter_finish(source, landing, sems):
        pltpu.make_async_copy(landing, landing, sems.at[1]).wait()
        return total(landing, NR)

    def spread_start(source, whole, sems):
        part = whole.at[pl.ds(pl.multiple_of(mine * tile, tile), tile)]
        pltpu.make_async_copy(source, part, sems.at[3]).start()

        def one(k, carry):
            pltpu.make_async_remote_copy(
                src_ref=source,
                dst_ref=part,
                send_sem=sems.at[2],
                recv_sem=sems.at[3],
                device_id=(lax.rem(me + k, NR), z),
                device_id_type=MESH,
            ).start()
            return carry

        lax.fori_loop(1, NR, one, 0)

    for copy in pan_copies:
        copy.wait()
    gram = None
    for h in range(PARTS):
        own = pan[z, h]
        part = contract_rows(own, own, HIGHEST)
        gram = part if gram is None else gram + part
    gram_local[...] = gram
    cacc[...] = jnp.zeros_like(cacc)
    meet(0)
    meet_line(0)
    for event in range(PARTS // 2, min(PARTS, events)):
        send(event, own=True)
    trl_copy.wait()
    for h in range(PARTS):
        multiply(z, h)
    meet(1)
    meet(2)
    handle_range(0, 1, forward=False)
    meet(3)
    scatter_start(gram_local, gram_terms, gram_sems)
    handle_range(1, 2, forward=False)
    forward_range(PARTS, PARTS + 1)
    handle_range(2, 3, forward=False)
    meet_line(1)

    @pl.when(is_owner)
    def _():
        gram_zsum[...] = scatter_finish(gram_local, gram_terms, gram_sems)
        pltpu.make_async_copy(gram_zsum, gram_z.at[z], gram_sems.at[5]).start()

        def one(k, carry):
            pltpu.make_async_remote_copy(
                src_ref=gram_zsum,
                dst_ref=gram_z.at[z],
                send_sem=gram_sems.at[4],
                recv_sem=gram_sems.at[5],
                device_id=(me, lax.rem(z + k, NZ)),
                device_id_type=MESH,
            ).start()
            return carry

        lax.fori_loop(1, NZ, one, 0)

    forward_range(PARTS + 1, PARTS + 3)
    handle_range(3, 6)

    @pl.when(is_owner)
    def _():
        pltpu.make_async_copy(gram_z, gram_z, gram_sems.at[5]).wait()
        gram_sum[...] = total(gram_z, NZ)
        spread_start(gram_sum, gram_whole, gram_sems)

    handle_range(6, 8)
    pltpu.make_async_copy(gram_whole, gram_whole, gram_sems.at[3]).wait()
    row_index = lax.broadcasted_iota(jnp.int32, (WIDTH, WIDTH), 0)
    column_index = lax.broadcasted_iota(jnp.int32, (WIDTH, WIDTH), 1)
    work[:, :WIDTH] = gram_whole[...]
    work[:, WIDTH:] = jnp.where(row_index == column_index, 1.0, 0.0).astype(jnp.float32)
    blocks = WIDTH // BLOCK

    def eliminate_part(part, carry):
        eliminate(work, part * (blocks // 4), blocks // 4)

        @pl.when(part + 8 < events)
        def _():
            handle(part + 8, True)

        return carry

    lax.fori_loop(0, 4, eliminate_part, 0)
    upper = jnp.where(row_index <= column_index, work[:, :WIDTH], 0.0)
    diagonal = jnp.sum(
        jnp.where(row_index == column_index, upper, 0.0), axis=1, keepdims=True
    )
    factor_out[...] = upper / jnp.sqrt(diagonal)
    work[:, WIDTH:] = work[:, WIDTH:] / jnp.sqrt(diagonal)
    twice(pair, work[:, WIDTH:].T)

    def to_basis(first, last):
        size = HB * PARTS // 2

        def one(index, carry):
            rows = pl.ds(pl.multiple_of(index * size, size), size)
            product = jnp.dot(terms[rows, :], pair[...], preferred_element_type=jnp.float32)
            terms[rows, :] = split_terms(product[:, :WIDTH] + product[:, WIDTH:])
            return carry

        lax.fori_loop(first, last, one, 0)

    handle_range(12, events, forward=False)

    moves = sorted(range(1, side), key=lambda move: -min(move, side - move))
    deep = WIDTH // 2
    first, second = prod_sems.at[0], prod_sems.at[1]
    along, across = jnp.where(core == 0, x, y), jnp.where(core == 0, y, x)
    sibling = device(y, x, 1 - core)

    def half(which):
        return pl.ds(pl.multiple_of(which * deep, deep), deep)

    def deliver(source, target, sems, peer):
        pltpu.make_async_remote_copy(
            src_ref=source,
            dst_ref=target,
            send_sem=sems.at[0],
            recv_sem=sems.at[1],
            device_id=(peer, z),
            device_id_type=MESH,
        ).start()

    for move in moves:
        along_x, along_y = lax.rem(x + move, side), lax.rem(y + move, side)
        deliver(cacc.at[:deep], line_terms.at[x * 2 + core], first, device(y, along_x, 0))
        deliver(cacc.at[deep:], line_terms.at[y * 2 + core], first, device(along_y, x, 1))
    deliver(cacc.at[half(1 - core)], line_terms.at[across * 2 + core], first, sibling)
    line_terms[along * 2 + core] = cacc[half(core), :]

    def ring_sent(event, carry):
        sent(pan.at[0, 0], right_send.at[event])
        sent(pan.at[0, 0], left_send.at[event])
        return carry

    lax.fori_loop(0, last, ring_sent, 0)
    sent(pan.at[0, 0], left_send.at[last])

    @pl.when(right != 0)
    def _():
        sent(pan.at[0, 0], right_send.at[last])

    @pl.when(right == 0)
    def _():
        sent(pan.at[0, 0, pl.ds(0, cut)], right_send.at[last])

    @pl.when(left == 0)
    def _():
        sent(pan.at[0, 0, pl.ds(cut, HB - cut)], left_send.at[events])

    @pl.when(is_owner)
    def _():
        sent(gram_local.at[: WIDTH - tile], gram_sems.at[0])
        sent(gram_terms.at[: NR - 1], gram_sems.at[2])
        sent(gram_z.at[: NZ - 1], gram_sems.at[4])

    @pl.when(jnp.logical_not(is_owner))
    def _():
        sent(gram_local, gram_sems.at[0])

    others = line_terms.at[: 2 * side - 1]
    to_basis(0, NZ)
    sent(others, first.at[1])
    half_sum[...] = total(line_terms, 2 * side)
    for move in moves:
        far_y = jnp.where(core == 0, lax.rem(y + move, side), y)
        far_x = jnp.where(core == 0, x, lax.rem(x + move, side))
        for which in range(2):
            deliver(half_sum, cross_terms.at[core, across], second, device(far_y, far_x, which))
    deliver(half_sum, cross_terms.at[core, across], second, sibling)
    cross_terms[core, across] = half_sum[...]
    sent(others, first.at[0])
    to_basis(NZ, 2 * NZ)
    sent(others, second.at[1])
    prod_whole[:deep, :] = total(cross_terms.at[0], side)
    prod_whole[deep:, :] = total(cross_terms.at[1], side)
    inverse_t = work[:, WIDTH:]
    coupling_out[...] = jnp.dot(
        inverse_t, prod_whole[...], precision=HIGHEST, preferred_element_type=jnp.float32
    )

    sent(others, second.at[0])


def apply_kernel(size, terms, trailing, factor, coupling, updated, factor_out, coupling_out, pair, held, sem, small_sem):
    factor_copy = pltpu.make_async_copy(factor, factor_out, small_sem.at[0])
    coupling_copy = pltpu.make_async_copy(coupling, coupling_out, small_sem.at[1])
    factor_copy.start()
    coupling_copy.start()
    twice(pair, coupling[...])
    for start in range(0, held.shape[0], size):
        rows = pl.ds(start, size)
        product = jnp.dot(terms[rows, :], pair[...], preferred_element_type=jnp.float32)
        held[rows, :] = trailing[rows, :] - (product[:, :WIDTH] + product[:, WIDTH:])
        pltpu.make_async_copy(held.at[rows], updated.at[rows], sem).start()
    pltpu.make_async_copy(held, updated, sem).wait()
    factor_copy.wait()
    coupling_copy.wait()


def per_device(NR, NZ, panel, trailing):
    HB = panel.shape[0] // PARTS
    rows = trailing.shape[0]
    owners = min(NR, 16)
    tile = WIDTH // owners
    events = ring_events(NZ)
    side = plane_side(NR)
    f32 = jnp.float32
    square = pltpu.VMEM((WIDTH, WIDTH), f32)
    small = jax.ShapeDtypeStruct((WIDTH, WIDTH), f32)
    kept_terms = pltpu.VMEM((rows, 2 * WIDTH), jnp.bfloat16)
    kept_rows = pltpu.VMEM((rows, WIDTH), f32)
    in_vmem = pl.BlockSpec(memory_space=pltpu.VMEM)
    anywhere = pl.BlockSpec(memory_space=pl.ANY)
    dma = pltpu.SemaphoreType.DMA
    factor, coupling, terms, kept = pl.pallas_call(
        functools.partial(main_kernel, NR, NZ, HB),
        out_shape=(square, square, kept_terms, kept_rows),
        in_specs=[anywhere, anywhere],
        out_specs=(in_vmem,) * 4,
        scratch_shapes=[
            pltpu.VMEM((NZ, PARTS, HB, WIDTH), f32),
            square,
            square,
            pltpu.VMEM((NR, tile, WIDTH), f32),
            pltpu.VMEM((NZ, tile, WIDTH), f32),
            pltpu.VMEM((tile, WIDTH), f32),
            pltpu.VMEM((tile, WIDTH), f32),
            square,
            pltpu.VMEM((2 * side, WIDTH // 2, WIDTH), f32),
            pltpu.VMEM((WIDTH // 2, WIDTH), f32),
            pltpu.VMEM((2, side, WIDTH // 2, WIDTH), f32),
            square,
            pltpu.VMEM((WIDTH, 2 * WIDTH), f32),
            pltpu.VMEM((2 * WIDTH, 2 * WIDTH), jnp.bfloat16),
            dma((PARTS,)),
            dma,
            dma((events + 1,)),
            dma((events + 1,)),
            dma((events + 1,)),
            dma((events + 1,)),
            dma((6,)),
            dma((2, 2)),
            pltpu.SemaphoreType.REGULAR((max(near_rounds(NR), 1),)),
            pltpu.SemaphoreType.REGULAR((2,)),
        ],
        compiler_params=pltpu.CompilerParams(
            collective_id=0, has_side_effects=True, vmem_limit_bytes=MAIN_VMEM
        ),
        name="gather_factor_couple",
    )(panel, trailing)
    updated, factor, coupling = pl.pallas_call(
        functools.partial(apply_kernel, min(rows, 128)),
        out_shape=(jax.ShapeDtypeStruct(trailing.shape, f32), small, small),
        in_specs=[in_vmem] * 4,
        out_specs=(anywhere,) * 3,
        scratch_shapes=[
            pltpu.VMEM((2 * WIDTH, 2 * WIDTH), jnp.bfloat16),
            pltpu.VMEM((rows, WIDTH), f32),
            dma,
            dma((2,)),
        ],
        compiler_params=pltpu.CompilerParams(vmem_limit_bytes=APPLY_VMEM),
        name="apply_update",
    )(terms, kept, factor, coupling)
    return factor, coupling, updated


def solution(mesh):
    return jax.shard_map(
        functools.partial(per_device, mesh.shape["rows"], mesh.shape["cols"]),
        mesh=mesh,
        in_specs=(P(("rows", "cols"), None), P("rows", "cols")),
        out_specs=(P(), P(None, "cols"), P("rows", "cols")),
        check_vma=False,
    )
```

```python
import functools

import jax
import jax.numpy as jnp
from jax import lax
from jax.experimental import pallas as pl
from jax.experimental.pallas import tpu as pltpu
from jax.sharding import PartitionSpec as P

MESH = pl.DeviceIdType.MESH
HIGHEST = lax.Precision.HIGHEST
WIDTH = 128
BLOCK = 8
PARTS = 4
MAIN_VMEM = 52 * 1024 * 1024
APPLY_VMEM = 16 * 1024 * 1024


def split_terms(value):
    high = value.astype(jnp.bfloat16)
    low = (value - high.astype(jnp.float32)).astype(jnp.bfloat16)
    return jnp.concatenate([high, low], axis=1)


def twice(pair, value):
    split = split_terms(value)
    pair[:WIDTH, :] = split
    pair[WIDTH:, :] = split


def contract_rows(left, right, precision=None):
    return lax.dot_general(
        left,
        right,
        (((0,), (0,)), ((), ())),
        precision=precision,
        preferred_element_type=jnp.float32,
    )


def eliminate(work, first, count):
    lane = lax.broadcasted_iota(jnp.int32, (BLOCK, WIDTH), 1)
    sub = lax.broadcasted_iota(jnp.int32, (BLOCK, WIDTH), 0)

    def one_block(index, carry):
        start = pl.multiple_of((first + index) * BLOCK, BLOCK)
        rows = work[pl.ds(start, BLOCK), :]
        gram_part = rows[:, :WIDTH]
        columns = []
        for a in range(BLOCK):
            picked = jnp.where(lane == start + a, gram_part, 0.0)
            column = jnp.sum(picked, axis=1, keepdims=True)
            columns.append(jnp.broadcast_to(column, (BLOCK, WIDTH)))
        scale = jnp.zeros((BLOCK, WIDTH), jnp.float32)
        for a in range(BLOCK):
            inverse = 1.0 / jnp.broadcast_to(columns[a][a : a + 1, :], (BLOCK, WIDTH))
            scale = jnp.where(sub == a, inverse, scale)
            factor = jnp.where(sub > a, columns[a] * inverse, 0.0)
            for d in range(a + 1, BLOCK):
                pivot_row = jnp.broadcast_to(columns[d][a : a + 1, :], (BLOCK, WIDTH))
                columns[d] = columns[d] - factor * pivot_row
            pivot_row = jnp.broadcast_to(rows[a : a + 1, :], (BLOCK, 2 * WIDTH))
            rows = rows - jnp.concatenate([factor, factor], axis=1) * pivot_row
        work[pl.ds(start, BLOCK), :] = rows
        lower = jnp.where(lane >= start + BLOCK, rows[:, :WIDTH] * scale, 0.0)
        work[...] = work[...] - contract_rows(lower, rows, HIGHEST)
        return carry

    lax.fori_loop(0, count, one_block, 0)


def plane_side(NR):
    side = 1
    while side * side * 2 < NR:
        side *= 2
    return side


def ring_events(NZ):
    return PARTS * (NZ // 2 - 1) + PARTS // 2


def near_rounds(NR):
    return 2 * (plane_side(NR) // 2)


def main_kernel(
    NR, NZ, HB,
    panel, trailing,
    factor_out, coupling_out, terms, trl,
    pan, cacc,
    gram_local, gram_terms, gram_z, gram_zsum, gram_sum, gram_whole,
    line_terms, half_sum, cross_terms, prod_whole, work, pair,
    pan_sem, trl_sem,
    right_send, right_recv, left_send, left_recv,
    gram_sems, prod_sems, near_sems, line_sems,
):
    me = lax.axis_index("rows")
    z = lax.axis_index("cols")
    owners = min(NR, 16)
    step = NR // owners
    tile = WIDTH // owners
    is_owner = lax.rem(me, step) == 0
    mine = me // step
    events = ring_events(NZ)
    right, left = lax.rem(z + 1, NZ), lax.rem(z + NZ - 1, NZ)

    side, core, chip = plane_side(NR), lax.rem(me, 2), me // 2
    x, y = lax.rem(chip, side), chip // side

    def device(row, column, which):
        return (row * side + column) * 2 + which

    line = [(me, right), (me, left)]
    neighbours = [(device(y, x, 1 - core), z)]
    if side > 1:
        for move in (1, side - 1):
            neighbours.append((device(y, lax.rem(x + move, side), core), z))
            neighbours.append((device(lax.rem(y + move, side), x, core), z))

    def greet(sem, devices):
        for other in devices:
            pl.semaphore_signal(sem, inc=1, device_id=other, device_id_type=MESH)

    def meet(k):
        if k < near_rounds(NR):
            pl.semaphore_wait(near_sems.at[k], len(neighbours))
            if k + 1 < near_rounds(NR):
                greet(near_sems.at[k + 1], neighbours)

    def meet_line(k):
        if NZ >= 4 * (k + 1):
            pl.semaphore_wait(line_sems.at[k], 2)
        if k == 0 and NZ >= 8:
            for move in (2, NZ - 2):
                greet(line_sems.at[1], [(me, lax.rem(z + move, NZ))])

    barrier = pltpu.get_barrier_semaphore()
    greet(barrier, line + neighbours)
    pan_copies = [
        pltpu.make_async_copy(panel.at[pl.ds(h * HB, HB)], pan.at[z, h], pan_sem.at[h])
        for h in range(PARTS)
    ]
    for copy in pan_copies:
        copy.start()
    trl_copy = pltpu.make_async_copy(trailing, trl, trl_sem)
    trl_copy.start()
    pl.semaphore_wait(barrier, len(line + neighbours))

    def place(event, back, to_right):
        part = event % PARTS
        if to_right:
            return lax.rem(z - event // PARTS - back + NZ, NZ), part
        return lax.rem(z + event // PARTS + back, NZ), PARTS - 1 - part

    def send(event, own=False):
        for to_right in (True, False):
            origin, slot = place(event, 0, to_right)
            here = pan.at[origin, slot]
            pltpu.make_async_remote_copy(
                src_ref=panel.at[pl.ds(slot * HB, HB)] if own else here,
                dst_ref=here,
                send_sem=(right_send if to_right else left_send).at[event],
                recv_sem=(right_recv if to_right else left_recv).at[event],
                device_id=(me, right if to_right else left),
                device_id_type=MESH,
            ).start()

    def sent(ref, sem):
        pltpu.make_async_copy(ref, ref, sem).wait()

    last, cut = events - 1, HB // 2

    def send_piece(event, to_right, first, count):
        origin, slot = place(event, 0, to_right)
        piece = pan.at[origin, slot, pl.ds(first, count)]
        pltpu.make_async_remote_copy(
            src_ref=piece,
            dst_ref=piece,
            send_sem=(right_send if to_right else left_send).at[event],
            recv_sem=(right_recv if to_right else left_recv).at[event],
            device_id=(me, right if to_right else left),
            device_id_type=MESH,
        ).start()

    def send_last():
        @pl.when(right != 0)
        def _():
            send_piece(last, True, 0, HB)

        @pl.when(right == 0)
        def _():
            send_piece(last, True, 0, cut)

        send_piece(last, False, 0, HB)

    def send_extra():
        @pl.when(left == 0)
        def _():
            send_piece(events, False, cut, HB - cut)

    if NZ >= 4:
        greet(line_sems.at[0], line)
    for event in range(PARTS // 2):
        send(event, own=True)
    if near_rounds(NR):
        greet(near_sems.at[0], neighbours)

    def rows_of(origin, slot):
        return pl.ds(pl.multiple_of((origin * PARTS + slot) * HB, HB), HB)

    def multiply(origin, slot):
        split = split_terms(pan[origin, slot])
        terms[rows_of(origin, slot), :] = split
        product = contract_rows(split, split_terms(trl[rows_of(origin, slot), :]))
        cacc[...] += (
            product[:WIDTH, :WIDTH] + product[WIDTH:, :WIDTH] + product[:WIDTH, WIDTH:]
        )

    def handle(event, forward):
        origin, slot = place(event, 1, True)
        split = jnp.logical_and(event == last, z == 0)

        @pl.when(jnp.logical_not(split))
        def _():
            sent(pan.at[origin, slot], right_recv.at[event])

        @pl.when(split)
        def _():
            sent(pan.at[origin, slot, pl.ds(0, cut)], right_recv.at[event])
            sent(pan.at[origin, slot, pl.ds(cut, HB - cut)], left_recv.at[events])

        origin, slot = place(event, 1, False)
        sent(pan.at[origin, slot], left_recv.at[event])
        if forward:

            @pl.when(event + PARTS < last)
            def _():
                send(event + PARTS)

            @pl.when(event + PARTS == last)
            def _():
                send_last()

            @pl.when(event + PARTS == events)
            def _():
                send_extra()

        for from_left in (True, False):
            multiply(*place(event, 1, from_left))

    def handle_range(first, stop, forward=True):
        def one(event, carry):
            handle(event, forward)
            return carry

        if first < min(stop, events):
            lax.fori_loop(first, min(stop, events), one, 0)

    def forward_range(first, stop):
        for event in range(first, min(stop, events + 1)):
            if event < last:
                send(event)
            elif event == last:
                send_last()
            else:
                send_extra()

    def scatter_start(source, landing, sems):
        def one(index, carry):
            owner = index * step
            part = source.at[pl.ds(pl.multiple_of(index * tile, tile), tile)]

            @pl.when(owner == me)
            def _():
                pltpu.make_async_copy(part, landing.at[me], sems.at[1]).start()

            @pl.when(owner != me)
            def _():
                pltpu.make_async_remote_copy(
                    src_ref=part,
                    dst_ref=landing.at[me],
                    send_sem=sems.at[0],
                    recv_sem=sems.at[1],
                    device_id=(owner, z),
                    device_id_type=MESH,
                ).start()

            return carry

        lax.fori_loop(0, owners, one, 0)

    def total(landing, count):
        value = landing[0]
        for k in range(1, count):
            value = value + landing[k]
        return value

    def scatter_finish(source, landing, sems):
        pltpu.make_async_copy(landing, landing, sems.at[1]).wait()
        return total(landing, NR)

    def spread_start(source, whole, sems):
        part = whole.at[pl.ds(pl.multiple_of(mine * tile, tile), tile)]
        pltpu.make_async_copy(source, part, sems.at[3]).start()

        def one(k, carry):
            pltpu.make_async_remote_copy(
                src_ref=source,
                dst_ref=part,
                send_sem=sems.at[2],
                recv_sem=sems.at[3],
                device_id=(lax.rem(me + k, NR), z),
                device_id_type=MESH,
            ).start()
            return carry

        lax.fori_loop(1, NR, one, 0)

    for copy in pan_copies:
        copy.wait()
    gram = None
    for h in range(PARTS):
        own = pan[z, h]
        part = contract_rows(own, own, HIGHEST)
        gram = part if gram is None else gram + part
    gram_local[...] = gram
    cacc[...] = jnp.zeros_like(cacc)
    meet(0)
    meet_line(0)
    for event in range(PARTS // 2, min(PARTS, events)):
        send(event, own=True)
    trl_copy.wait()
    for h in range(PARTS):
        multiply(z, h)
    meet(1)
    meet(2)
    handle_range(0, 1, forward=False)
    meet(3)
    scatter_start(gram_local, gram_terms, gram_sems)
    handle_range(1, 2, forward=False)
    forward_range(PARTS, PARTS + 1)
    handle_range(2, 3, forward=False)
    meet_line(1)

    @pl.when(is_owner)
    def _():
        gram_zsum[...] = scatter_finish(gram_local, gram_terms, gram_sems)
        pltpu.make_async_copy(gram_zsum, gram_z.at[z], gram_sems.at[5]).start()

        def one(k, carry):
            pltpu.make_async_remote_copy(
                src_ref=gram_zsum,
                dst_ref=gram_z.at[z],
                send_sem=gram_sems.at[4],
                recv_sem=gram_sems.at[5],
                device_id=(me, lax.rem(z + k, NZ)),
                device_id_type=MESH,
            ).start()
            return carry

        lax.fori_loop(1, NZ, one, 0)

    forward_range(PARTS + 1, PARTS + 3)
    handle_range(3, 6)

    @pl.when(is_owner)
    def _():
        pltpu.make_async_copy(gram_z, gram_z, gram_sems.at[5]).wait()
        gram_sum[...] = total(gram_z, NZ)
        spread_start(gram_sum, gram_whole, gram_sems)

    handle_range(6, 8)
    pltpu.make_async_copy(gram_whole, gram_whole, gram_sems.at[3]).wait()
    row_index = lax.broadcasted_iota(jnp.int32, (WIDTH, WIDTH), 0)
    column_index = lax.broadcasted_iota(jnp.int32, (WIDTH, WIDTH), 1)
    work[:, :WIDTH] = gram_whole[...]
    work[:, WIDTH:] = jnp.where(row_index == column_index, 1.0, 0.0).astype(jnp.float32)
    blocks = WIDTH // BLOCK

    def eliminate_part(part, carry):
        eliminate(work, part * (blocks // 4), blocks // 4)

        @pl.when(part + 8 < events)
        def _():
            handle(part + 8, True)

        return carry

    lax.fori_loop(0, 4, eliminate_part, 0)
    upper = jnp.where(row_index <= column_index, work[:, :WIDTH], 0.0)
    diagonal = jnp.sum(
        jnp.where(row_index == column_index, upper, 0.0), axis=1, keepdims=True
    )
    factor_out[...] = upper / jnp.sqrt(diagonal)
    work[:, WIDTH:] = work[:, WIDTH:] / jnp.sqrt(diagonal)
    twice(pair, work[:, WIDTH:].T)

    def to_basis(first, last):
        size = HB * PARTS // 2

        def one(index, carry):
            rows = pl.ds(pl.multiple_of(index * size, size), size)
            product = jnp.dot(terms[rows, :], pair[...], preferred_element_type=jnp.float32)
            terms[rows, :] = split_terms(product[:, :WIDTH] + product[:, WIDTH:])
            return carry

        lax.fori_loop(first, last, one, 0)

    handle_range(12, events, forward=False)

    moves = sorted(range(1, side), key=lambda move: -min(move, side - move))
    deep = WIDTH // 2
    first, second = prod_sems.at[0], prod_sems.at[1]
    along, across = jnp.where(core == 0, x, y), jnp.where(core == 0, y, x)
    sibling = device(y, x, 1 - core)

    def half(which):
        return pl.ds(pl.multiple_of(which * deep, deep), deep)

    def deliver(source, target, sems, peer):
        pltpu.make_async_remote_copy(
            src_ref=source,
            dst_ref=target,
            send_sem=sems.at[0],
            recv_sem=sems.at[1],
            device_id=(peer, z),
            device_id_type=MESH,
        ).start()

    for move in moves:
        along_x, along_y = lax.rem(x + move, side), lax.rem(y + move, side)
        deliver(cacc.at[:deep], line_terms.at[x * 2 + core], first, device(y, along_x, 0))
        deliver(cacc.at[deep:], line_terms.at[y * 2 + core], first, device(along_y, x, 1))
    deliver(cacc.at[half(1 - core)], line_terms.at[across * 2 + core], first, sibling)
    line_terms[along * 2 + core] = cacc[half(core), :]

    def ring_sent(event, carry):
        sent(pan.at[0, 0], right_send.at[event])
        sent(pan.at[0, 0], left_send.at[event])
        return carry

    lax.fori_loop(0, last, ring_sent, 0)
    sent(pan.at[0, 0], left_send.at[last])

    @pl.when(right != 0)
    def _():
        sent(pan.at[0, 0], right_send.at[last])

    @pl.when(right == 0)
    def _():
        sent(pan.at[0, 0, pl.ds(0, cut)], right_send.at[last])

    @pl.when(left == 0)
    def _():
        sent(pan.at[0, 0, pl.ds(cut, HB - cut)], left_send.at[events])

    @pl.when(is_owner)
    def _():
        sent(gram_local.at[: WIDTH - tile], gram_sems.at[0])
        sent(gram_terms.at[: NR - 1], gram_sems.at[2])
        sent(gram_z.at[: NZ - 1], gram_sems.at[4])

    @pl.when(jnp.logical_not(is_owner))
    def _():
        sent(gram_local, gram_sems.at[0])

    others = line_terms.at[: 2 * side - 1]
    to_basis(0, NZ)
    sent(others, first.at[1])
    half_sum[...] = total(line_terms, 2 * side)
    for move in moves:
        far_y = jnp.where(core == 0, lax.rem(y + move, side), y)
        far_x = jnp.where(core == 0, x, lax.rem(x + move, side))
        for which in range(2):
            deliver(half_sum, cross_terms.at[core, across], second, device(far_y, far_x, which))
    deliver(half_sum, cross_terms.at[core, across], second, sibling)
    cross_terms[core, across] = half_sum[...]
    sent(others, first.at[0])
    to_basis(NZ, 2 * NZ)
    sent(others, second.at[1])
    prod_whole[:deep, :] = total(cross_terms.at[0], side)
    prod_whole[deep:, :] = total(cross_terms.at[1], side)
    inverse_t = work[:, WIDTH:]
    coupling_out[...] = jnp.dot(
        inverse_t, prod_whole[...], precision=HIGHEST, preferred_element_type=jnp.float32
    )

    sent(others, second.at[0])


def apply_kernel(size, terms, trailing, factor, coupling, updated, factor_out, coupling_out, pair, held, sem, small_sem):
    factor_copy = pltpu.make_async_copy(factor, factor_out, small_sem.at[0])
    coupling_copy = pltpu.make_async_copy(coupling, coupling_out, small_sem.at[1])
    factor_copy.start()
    coupling_copy.start()
    twice(pair, coupling[...])
    for start in range(0, held.shape[0], size):
        rows = pl.ds(start, size)
        product = jnp.dot(terms[rows, :], pair[...], preferred_element_type=jnp.float32)
        held[rows, :] = trailing[rows, :] - (product[:, :WIDTH] + product[:, WIDTH:])
        pltpu.make_async_copy(held.at[rows], updated.at[rows], sem).start()
    pltpu.make_async_copy(held, updated, sem).wait()
    factor_copy.wait()
    coupling_copy.wait()


def per_device(NR, NZ, panel, trailing):
    HB = panel.shape[0] // PARTS
    rows = trailing.shape[0]
    owners = min(NR, 16)
    tile = WIDTH // owners
    events = ring_events(NZ)
    side = plane_side(NR)
    f32 = jnp.float32
    square = pltpu.VMEM((WIDTH, WIDTH), f32)
    small = jax.ShapeDtypeStruct((WIDTH, WIDTH), f32)
    kept_terms = pltpu.VMEM((rows, 2 * WIDTH), jnp.bfloat16)
    kept_rows = pltpu.VMEM((rows, WIDTH), f32)
    in_vmem = pl.BlockSpec(memory_space=pltpu.VMEM)
    anywhere = pl.BlockSpec(memory_space=pl.ANY)
    dma = pltpu.SemaphoreType.DMA
    factor, coupling, terms, kept = pl.pallas_call(
        functools.partial(main_kernel, NR, NZ, HB),
        out_shape=(square, square, kept_terms, kept_rows),
        in_specs=[anywhere, anywhere],
        out_specs=(in_vmem,) * 4,
        scratch_shapes=[
            pltpu.VMEM((NZ, PARTS, HB, WIDTH), f32),
            square,
            square,
            pltpu.VMEM((NR, tile, WIDTH), f32),
            pltpu.VMEM((NZ, tile, WIDTH), f32),
            pltpu.VMEM((tile, WIDTH), f32),
            pltpu.VMEM((tile, WIDTH), f32),
            square,
            pltpu.VMEM((2 * side, WIDTH // 2, WIDTH), f32),
            pltpu.VMEM((WIDTH // 2, WIDTH), f32),
            pltpu.VMEM((2, side, WIDTH // 2, WIDTH), f32),
            square,
            pltpu.VMEM((WIDTH, 2 * WIDTH), f32),
            pltpu.VMEM((2 * WIDTH, 2 * WIDTH), jnp.bfloat16),
            dma((PARTS,)),
            dma,
            dma((events + 1,)),
            dma((events + 1,)),
            dma((events + 1,)),
            dma((events + 1,)),
            dma((6,)),
            dma((2, 2)),
            pltpu.SemaphoreType.REGULAR((max(near_rounds(NR), 1),)),
            pltpu.SemaphoreType.REGULAR((2,)),
        ],
        compiler_params=pltpu.CompilerParams(
            collective_id=0, has_side_effects=True, vmem_limit_bytes=MAIN_VMEM
        ),
        name="gather_factor_couple",
    )(panel, trailing)
    updated, factor, coupling = pl.pallas_call(
        functools.partial(apply_kernel, min(rows, 64)),
        out_shape=(jax.ShapeDtypeStruct(trailing.shape, f32), small, small),
        in_specs=[in_vmem] * 4,
        out_specs=(anywhere,) * 3,
        scratch_shapes=[
            pltpu.VMEM((2 * WIDTH, 2 * WIDTH), jnp.bfloat16),
            pltpu.VMEM((rows, WIDTH), f32),
            dma,
            dma((2,)),
        ],
        compiler_params=pltpu.CompilerParams(vmem_limit_bytes=APPLY_VMEM),
        name="apply_update",
    )(terms, kept, factor, coupling)
    return factor, coupling, updated


def solution(mesh):
    return jax.shard_map(
        functools.partial(per_device, mesh.shape["rows"], mesh.shape["cols"]),
        mesh=mesh,
        in_specs=(P(("rows", "cols"), None), P("rows", "cols")),
        out_specs=(P(), P(None, "cols"), P("rows", "cols")),
        check_vma=False,
    )
```
